256 devices in a mesh: leaf: 256 (over x, z, y, core).
Axes of the slice: x: 4, y: 4, z: 8, core: 2. Of those that a mesh axis runs over, the one named last changes fastest.
Arguments:
- values: float32 [32, 2097152], P(None, 'leaf'), may hold values from -6 to 6
- points: float32 [3, 2097152], P(None, 'leaf'), as said below
- basis: float32 [64, 2097152], P(None, 'leaf'), may hold values from -0.5 to 0.5
- local_transfer: float32 [16128, 64, 128], P('leaf'), may hold values from -0.625 to 0.625
- local_coupling: float32 [32256, 64, 128], P('leaf'), may hold values from -0.5 to 0.5
- local_partners: int32 [32256, 2], P('leaf'), may hold values from 0 to 16383, as said below
- top_transfer: float32 [7, 64, 128], replicated, may hold values from -0.625 to 0.625
- top_coupling: float32 [8, 64, 128], replicated, may hold values from -0.75 to 0.75
- near_cols: int32 [16384, 8], P('leaf'), may hold values from 0 to 16383, as said below
- near_count: int32 [16384], P('leaf'), may hold values from 1 to 8, as said below
Outputs:
- product: float32 [32, 2097152], P(None, 'leaf')
The draws below stay inside these ranges and needn't reach their ends.
Inputs may be any that keep to these rules, and one draw needn't show every extreme that they name: `points`: point p lies in the unit cube of leaf n = p // 128. With d = n // 64 and l = n mod 64, the cube's lowest corner is l decoded in Morton order (bits 3j, 3j + 1, 3j + 2 give bit j of the first, second and third coordinate), moved along the first coordinate by d * 2^(2): the blocks of consecutive 64 leaves lie side by side along the first coordinate. `near_cols`: row g lists leaves whose cubes touch leaf g's cube and whose indices differ from g by at most 64; the first entry is g itself. `near_count`: at most the number of distinct leaves in the row of near_cols. `local_partners`: the row of node i of level h (numbered as in the reference program) holds 2 distinct nodes of level h other than i, inside the window of 2w + 1 nodes centred on i and moved inward at the ends of the level, w = min(4, 64 / 2^(h+1)).
All inputs are finite; a program needn't handle non-finite values.
Results may differ from the reference program's by a relative error of at most 0.0003.
Values sent between devices are 32-bit elements; how exact they have to be, the bound alone decides.
A program may use at most 128 MiB of HBM per device.

```python
import jax
import jax.numpy as jnp
from jax import lax

LEAF_PTS = 128
RANK = 64
RHS = 32
NEAR_SLOTS = 8
COUPLE = 2
WINDOW = 4
LOC_LEVELS = 6
LEAVES_DEV = 64
TOP_LEVELS = 8
LEAVES = 16384
POINTS = 2097152
LOC_PARENTS = 16128
LOC_NODES = 32256
N_LEAF = 256


def morton_split(codes):
    along_x = jnp.zeros_like(codes)
    along_y = jnp.zeros_like(codes)
    along_z = jnp.zeros_like(codes)
    for bit_pos in range(8):
        along_x = along_x | (codes >> 3 * bit_pos & 1) << bit_pos
        along_y = along_y | (codes >> 3 * bit_pos + 1 & 1) << bit_pos
        along_z = along_z | (codes >> 3 * bit_pos + 2 & 1) << bit_pos
    return (along_x, along_y, along_z)


def morton_join(along_x, along_y, along_z):
    codes = jnp.zeros_like(along_x)
    for bit_pos in range(8):
        codes = codes | (along_x >> bit_pos & 1) << 3 * bit_pos
        codes = codes | (along_y >> bit_pos & 1) << 3 * bit_pos + 1
        codes = codes | (along_z >> bit_pos & 1) << 3 * bit_pos + 2
    return codes


def block_extent():
    return (2 ** ((LOC_LEVELS + 2) // 3), 2 ** ((LOC_LEVELS + 1) // 3), 2 ** (LOC_LEVELS // 3))


def leaf_corner(leaf_rows):
    extent_x, extent_y, extent_z = block_extent()
    device_id = leaf_rows // LEAVES_DEV
    grid_x, grid_y, grid_z = morton_split(leaf_rows % LEAVES_DEV)
    return (grid_x + device_id * extent_x, grid_y, grid_z)


def near_lists(key):
    extent_x, extent_y, extent_z = block_extent()
    device_total = LEAVES // LEAVES_DEV
    leaf_rows = jnp.arange(LEAVES, dtype=jnp.int32)
    grid_x, grid_y, grid_z = leaf_corner(leaf_rows)
    own_device = leaf_rows // LEAVES_DEV
    candidates = []
    allowed = []
    crossing = []
    for step_x in (-1, 0, 1):
        for step_y in (-1, 0, 1):
            for step_z in (-1, 0, 1):
                if not (step_x == 0 and step_y == 0 and (step_z == 0)):
                    moved_x = grid_x + step_x
                    moved_y = grid_y + step_y
                    moved_z = grid_z + step_z
                    inside = (moved_x >= 0) & (moved_y >= 0) & (moved_z >= 0)
                    inside = inside & (moved_y < extent_y) & (moved_z < extent_z) & (moved_x < device_total * extent_x)
                    safe_x = jnp.maximum(moved_x, 0)
                    other_device = safe_x // extent_x
                    codes = other_device * LEAVES_DEV + morton_join(safe_x % extent_x, jnp.clip(moved_y, 0, extent_y - 1), jnp.clip(moved_z, 0, extent_z - 1))
                    inside = inside & (jnp.abs(codes - leaf_rows) <= LEAVES_DEV)
                    candidates.append(codes)
                    allowed.append(inside)
                    crossing.append(inside & (other_device != own_device))
    candidates = jnp.stack(candidates, axis=1)
    allowed = jnp.stack(allowed, axis=1)
    crossing = jnp.stack(crossing, axis=1)
    slot_ids = jnp.arange(26, dtype=jnp.int32)
    scores = jax.random.randint(key, (LEAVES, 26), 0, 1 << 20, dtype=jnp.int32) * 32 + slot_ids[None, :]
    scores = scores + crossing.astype(jnp.int32) * (1 << 26)
    scores = jnp.where(allowed, scores, -1 - slot_ids[None, :])
    ranked, position = lax.top_k(scores, NEAR_SLOTS - 1)
    picked = jnp.take_along_axis(candidates, position, axis=1)
    picked = jnp.where(ranked >= 0, picked, leaf_rows[:, None])
    columns = jnp.concatenate([leaf_rows[:, None], picked], axis=1).astype(jnp.int32)
    usable = jnp.minimum(1 + jnp.sum(allowed.astype(jnp.int32), axis=1), NEAR_SLOTS)
    cross_picked = jnp.sum((ranked >= 1 << 26).astype(jnp.int32), axis=1)
    lowest = jnp.minimum(1 + cross_picked, usable)
    counts = jax.random.randint(jax.random.fold_in(key, 11), (LEAVES,), lowest, usable + 1, dtype=jnp.int32)
    return (columns, counts.astype(jnp.int32))


def draw_near_cols(key, part):
    columns, counts = near_lists(key)
    return columns


def draw_near_count(key, part):
    columns, counts = near_lists(key)
    return counts


def draw_points(key, part):
    key = jax.random.fold_in(key, 5)
    leaf_rows = jnp.arange(POINTS, dtype=jnp.int32) // LEAF_PTS
    grid_x, grid_y, grid_z = leaf_corner(leaf_rows)
    corner = jnp.stack([grid_x, grid_y, grid_z], axis=0).astype(jnp.float32)
    jitter = jax.random.uniform(key, (3, POINTS), jnp.float32)
    return corner + jitter


def draw_local_partners(key, part):
    key = jax.random.fold_in(key, 7)
    per_device = 2 * LEAVES_DEV - 2
    row_ids = jnp.arange(LOC_NODES, dtype=jnp.int32)
    device_id = row_ids // per_device
    inner = row_ids % per_device
    height = jnp.zeros_like(inner)
    for level_id in range(1, LOC_LEVELS):
        height = height + (inner >= 2 * LEAVES_DEV - 2 * (LEAVES_DEV >> level_id)).astype(jnp.int32)
    node_count = jnp.right_shift(jnp.full_like(inner, LEAVES_DEV), height)
    offset = 2 * LEAVES_DEV - 2 * node_count
    node = device_id * node_count + inner - offset
    level_total = LOC_NODES // per_device * node_count
    rim_width = jnp.minimum(WINDOW, node_count // 2)
    start_at = jnp.clip(node - rim_width, 0, level_total - 2 * rim_width - 1)
    slot_ids = jnp.arange(2 * WINDOW + 1, dtype=jnp.int32)
    candidates = start_at[:, None] + slot_ids[None, :]
    allowed = (slot_ids[None, :] <= 2 * rim_width[:, None]) & (candidates != node[:, None])
    scores = jax.random.randint(key, (LOC_NODES, 2 * WINDOW + 1), 0, 1 << 20, dtype=jnp.int32) * 32 + slot_ids[None, :]
    scores = jnp.where(allowed, scores, -1 - slot_ids[None, :])
    ranked, position = lax.top_k(scores, COUPLE)
    return jnp.take_along_axis(candidates, position, axis=1).astype(jnp.int32)


def steps_of(own_key, shape, pieces, smallest, largest):
    factor_of = 1.0
    for dim, blocks in pieces:
        heights = jax.random.uniform(jax.random.fold_in(jax.random.fold_in(own_key, 6), dim), (blocks,), jnp.float32, smallest / len(pieces), largest / len(pieces))
        factor_of = factor_of * jnp.repeat(jnp.exp(heights), shape[dim] // blocks).reshape((-1,) + (1,) * (len(shape) - 1 - dim))
    return factor_of


def gaussian(key, dims, deviation, bound, split=(), kind=jnp.bfloat16):
    array = deviation * jax.random.normal(key, dims, jnp.float32)
    if split:
        array = array * steps_of(key, dims, split, -0.22, 0.18)
    return jnp.clip(array, -bound, bound).astype(kind)


def setup_inputs(seed: int = 0) -> dict:
    key_list = jax.random.split(jax.random.key(seed), 11)
    values = gaussian(key_list[0], (RHS, POINTS), 1.0, 6.0, ((1, 256),), jnp.float32)
    points = draw_points(jax.random.fold_in(key_list[10], 71), 0)
    basis = gaussian(key_list[2], (RANK, POINTS), LEAF_PTS ** -0.5, 0.5, ((1, 256),), jnp.float32)
    local_transfer = gaussian(key_list[3], (LOC_PARENTS, RANK, 2 * RANK), ((RANK * 17) // 12) ** -0.5, 0.625, ((0, 256),), jnp.float32)
    local_coupling = gaussian(key_list[4], (LOC_NODES, RANK, COUPLE * RANK), (COUPLE * RANK) ** -0.5, 0.5, ((0, 256),), jnp.float32)
    local_partners = draw_local_partners(jax.random.fold_in(key_list[10], 71), 0)
    top_transfer = gaussian(key_list[6], (TOP_LEVELS - 1, RANK, 2 * RANK), ((RANK * 17) // 12) ** -0.5, 0.625, (), jnp.float32)
    top_coupling = gaussian(key_list[7], (TOP_LEVELS, RANK, 2 * RANK), RANK ** -0.5, 0.75, (), jnp.float32)
    near_cols = draw_near_cols(jax.random.fold_in(key_list[10], 71), 0)
    near_count = draw_near_count(jax.random.fold_in(key_list[10], 71), 0)
    return dict(values=values, points=points, basis=basis, local_transfer=local_transfer, local_coupling=local_coupling, local_partners=local_partners, top_transfer=top_transfer, top_coupling=top_coupling, near_cols=near_cols, near_count=near_count)


length_scale = 0.5
amplitude = 0.25
root_three = 1.7320508075688772
highest = lax.Precision.HIGHEST

def matern(target, source):
    along_x = target[0][:, None, :, None] - source[0][:, :, None, :]
    along_y = target[1][:, None, :, None] - source[1][:, :, None, :]
    along_z = target[2][:, None, :, None] - source[2][:, :, None, :]
    radius = jnp.sqrt(along_x * along_x + along_y * along_y + along_z * along_z)
    scaled = radius * (root_three / length_scale)
    return amplitude * (1.0 + scaled) * jnp.exp(-scaled)

def join_pairs(nodes):
    node_total = nodes.shape[0] // 2
    return nodes.reshape(node_total, 2, nodes.shape[1], nodes.shape[2]).transpose(0, 2, 1, 3).reshape(node_total, nodes.shape[1], 2 * nodes.shape[2])

def split_pairs(joined):
    node_total = joined.shape[0]
    half_rank = joined.shape[2] // 2
    return joined.reshape(node_total, joined.shape[1], 2, half_rank).transpose(0, 2, 1, 3).reshape(2 * node_total, joined.shape[1], half_rank)

def reference(values, points, basis, local_transfer, local_coupling, local_partners, top_transfer, top_coupling, near_cols, near_count):
    devices = N_LEAF
    levels_top = devices.bit_length() - 1
    rhs_blocks = values.reshape(RHS, LEAVES, LEAF_PTS)
    point_blocks = points.reshape(3, LEAVES, LEAF_PTS)
    leaf_bases = basis.reshape(RANK, LEAVES, LEAF_PTS)
    live_slots = (jnp.arange(NEAR_SLOTS)[None, :] < near_count[:, None]).astype(jnp.float32)

    def near_group(group_id):
        leaf_rows = group_id * LEAVES_DEV + jnp.arange(LEAVES_DEV)
        columns = near_cols[leaf_rows]
        target = point_blocks[:, leaf_rows]
        source = jnp.take(point_blocks, columns, axis=1)
        kernel = matern(target, source) * live_slots[leaf_rows][:, :, None, None]
        rhs_near = jnp.take(rhs_blocks, columns, axis=1)
        return jnp.einsum('gsmn,rgsn->rgm', kernel, rhs_near, precision=highest)
    near_part = lax.map(near_group, jnp.arange(devices))
    near_part = near_part.transpose(1, 0, 2, 3).reshape(RHS, LEAVES * LEAF_PTS)
    transfer_dev = local_transfer.reshape(devices, LEAVES_DEV - 1, RANK, 2 * RANK)
    coefficients = [jnp.einsum('rlm,klm->lrk', rhs_blocks, leaf_bases, precision=highest)]
    for height in range(1, LOC_LEVELS + 1):
        node_count = LEAVES_DEV >> height
        offset = LEAVES_DEV - 2 * node_count
        weights = transfer_dev[:, offset:offset + node_count].reshape(devices * node_count, RANK, 2 * RANK)
        coefficients.append(jnp.einsum('nrj,nkj->nrk', join_pairs(coefficients[-1]), weights, precision=highest))
    for step in range(levels_top - 1):
        coefficients.append(jnp.einsum('nrj,kj->nrk', join_pairs(coefficients[-1]), top_transfer[step], precision=highest))
    partners_dev = local_partners.reshape(devices, 2 * LEAVES_DEV - 2, COUPLE)
    coupling_dev = local_coupling.reshape(devices, 2 * LEAVES_DEV - 2, RANK, COUPLE * RANK)
    incoming = []
    for height in range(LOC_LEVELS):
        node_count = LEAVES_DEV >> height
        offset = 2 * LEAVES_DEV - 2 * node_count
        partners = partners_dev[:, offset:offset + node_count].reshape(devices * node_count, COUPLE)
        matrices = coupling_dev[:, offset:offset + node_count].reshape(devices * node_count, RANK, COUPLE * RANK)
        gathered = jnp.take(coefficients[height], partners, axis=0)
        gathered = gathered.transpose(0, 2, 1, 3).reshape(devices * node_count, RHS, COUPLE * RANK)
        incoming.append(jnp.einsum('nrj,nkj->nrk', gathered, matrices, precision=highest))
    for step in range(levels_top):
        nodes = coefficients[LOC_LEVELS + step]
        paired = nodes.reshape(nodes.shape[0] // 2, 2, RHS, RANK)
        even_side = jnp.einsum('prj,kj->prk', paired[:, 1], top_coupling[step][:, :RANK], precision=highest)
        odd_side = jnp.einsum('prj,kj->prk', paired[:, 0], top_coupling[step][:, RANK:], precision=highest)
        incoming.append(jnp.stack([even_side, odd_side], axis=1).reshape(nodes.shape[0], RHS, RANK))
    downward = incoming[-1]
    for step in reversed(range(levels_top - 1)):
        spread = jnp.einsum('nrk,kj->nrj', downward, top_transfer[step], precision=highest)
        downward = split_pairs(spread) + incoming[LOC_LEVELS + step]
    for height in range(LOC_LEVELS, 0, -1):
        node_count = LEAVES_DEV >> height
        offset = LEAVES_DEV - 2 * node_count
        weights = transfer_dev[:, offset:offset + node_count].reshape(devices * node_count, RANK, 2 * RANK)
        spread = jnp.einsum('nrk,nkj->nrj', downward, weights, precision=highest)
        downward = split_pairs(spread) + incoming[height - 1]
    far_part = jnp.einsum('lrk,klm->rlm', downward, leaf_bases, precision=highest).reshape(RHS, LEAVES * LEAF_PTS)
    return near_part + far_part
```

```python
import functools
import math

import jax
import jax.numpy as jnp
import numpy as np
from jax import lax
from jax.experimental import pallas as pl
from jax.experimental.pallas import tpu as pltpu
from jax.sharding import PartitionSpec as P

LEAF_PTS = 128
RANK = 64
RHS = 32
NEAR_SLOTS = 8
COUPLE = 2
WINDOW = 4
LOC_LEVELS = 6
LEAVES_DEV = 64
FACE = 16
SOURCES = LEAVES_DEV + 2 * FACE
ROUND_BITS = 4
BLOCKS = 8

MESH = pl.DeviceIdType.MESH
bf16 = jnp.bfloat16
f32 = jnp.float32
LOG2E = 1.4426950408889634
SCALE = math.sqrt(3.0) / 0.5 * LOG2E
AMPLITUDE = 0.25 / LOG2E

COUNTS = [LEAVES_DEV >> h for h in range(LOC_LEVELS + 1)]
RIMS = [min(WINDOW, (LEAVES_DEV >> h) // 2) for h in range(LOC_LEVELS)]
PAIR_AT = [LEAVES_DEV - COUNTS[h] for h in range(LOC_LEVELS)]
RIM_PAIRS = [max(1, r // 2) for r in RIMS]
RIM_AT = [sum(RIM_PAIRS[:h]) for h in range(LOC_LEVELS)]
WIDE_AT = [sum(COUNTS[g] + 2 * RIMS[g] for g in range(h)) for h in range(LOC_LEVELS + 1)]
TRANSFER_AT = [LEAVES_DEV - 2 * c for c in COUNTS]
COUPLING_AT = [2 * LEAVES_DEV - 2 * c for c in COUNTS]


def rounds_of(devices):
    total = devices.bit_length() - 1
    return [(b, min(ROUND_BITS, total - b)) for b in range(0, total, ROUND_BITS)]


def halves(a):
    high = a.astype(bf16)
    return high, (a - high.astype(f32)).astype(bf16)


def product(left, right, right_dim):
    dims = (((1,), (right_dim,)), ((), ()))
    left_high, left_low = halves(left)
    right_high, right_low = halves(right)
    rows = left.shape[0]
    both = lax.dot_general(
        jnp.concatenate([left_high, left_low], axis=0),
        right_high,
        dims,
        preferred_element_type=f32,
    )
    rest = lax.dot_general(left_high, right_low, dims, preferred_element_type=f32)
    return both[:rows] + (both[rows:] + rest)


def times_t(left, right):
    return product(left, right, 1)


def times(left, right):
    return product(left, right, 0)


def face_leaf(side, e):
    spread = ((e & 3) << 1) | ((e >> 2) << 4)
    return spread + 9 * side


def tree_kernel(
    devices,
    values_h,
    points_h,
    basis_h,
    transfer_h,
    coupling_h,
    top_transfer_h,
    top_coupling_h,
    partners,
    far,
    halo_x,
    halo_p,
    values,
    points,
    basis,
    transfer,
    coupling,
    top_transfer,
    top_coupling,
    face_x,
    face_p,
    pairs,
    rim,
    wide,
    field,
    down,
    packed,
    gathered,
    load_sem,
    face_send,
    face_recv,
    rim_ssem,
    rim_rsem,
    top_send,
    top_recv,
):
    me = lax.axis_index("leaf")
    right = lax.rem(me + 1, devices)
    left = lax.rem(me + devices - 1, devices)
    rounds = rounds_of(devices)
    levels_top = devices.bit_length() - 1

    barrier = pltpu.get_barrier_semaphore()
    greeted = 0
    for other in (left, right):
        pl.semaphore_signal(barrier, inc=1, device_id=(other,), device_id_type=MESH)
        greeted += 1
    for base, bits in rounds:
        for k in range(1, 1 << bits):
            pl.semaphore_signal(
                barrier, inc=1, device_id=(me ^ (k << base),), device_id_type=MESH
            )
            greeted += 1

    loads = []
    for n, (src, dst) in enumerate(
        [
            (values_h, values),
            (points_h, points),
            (basis_h, basis),
            (transfer_h, transfer),
            (coupling_h, coupling),
            (top_transfer_h, top_transfer),
            (top_coupling_h, top_coupling),
        ]
    ):
        copy = pltpu.make_async_copy(src, dst, load_sem.at[n])
        copy.start()
        loads.append(copy)

    lane_high = lax.broadcasted_iota(jnp.int32, (RHS, 2 * RANK), 1) >= RANK

    def join(out):
        return jnp.where(lane_high, out[RHS:], out[:RHS])

    loads[0].wait()
    loads[1].wait()
    for side in range(2):
        for e in range(FACE):
            leaf = face_leaf(1 - side, e)
            at = leaf * LEAF_PTS
            face_x[side, e] = values[:, at : at + LEAF_PTS]
            for axis in range(3):
                face_p[side, axis, e : e + 1, :] = points[axis : axis + 1, at : at + LEAF_PTS]
    pl.semaphore_wait(barrier, greeted)
    face_copies = []
    for side, other in ((0, right), (1, left)):
        for n, (src, dst) in enumerate(((face_x, halo_x), (face_p, halo_p))):
            copy = pltpu.make_async_remote_copy(
                src_ref=src.at[side],
                dst_ref=dst.at[side],
                send_sem=face_send.at[side, n],
                recv_sem=face_recv.at[side, n],
                device_id=(other,),
                device_id_type=MESH,
            )
            copy.start()
            face_copies.append(copy)

    rim_copies = [[] for _ in range(LOC_LEVELS)]

    def send_rim(h):
        count = RIM_PAIRS[h]
        at = RIM_AT[h]
        first = PAIR_AT[h]
        last = first + COUNTS[h] // 2 - count
        for side, (other, start) in enumerate(((right, last), (left, first))):
            copy = pltpu.make_async_remote_copy(
                src_ref=pairs.at[pl.ds(start, count)],
                dst_ref=rim.at[side, pl.ds(at, count)],
                send_sem=rim_ssem.at[side, h],
                recv_sem=rim_rsem.at[side, h],
                device_id=(other,),
                device_id_type=MESH,
            )
            copy.start()
            rim_copies[h].append(copy)

    def widen(h, slot, pair, which):
        turned = pltpu.roll(pair, RANK, 1)
        if which != 1:
            wide[WIDE_AT[h] + slot] = jnp.where(lane_high, turned, pair)
        if which != 0:
            wide[WIDE_AT[h] + slot + (which == 2)] = jnp.where(lane_high, pair, turned)

    loads[2].wait()

    def leaf_pair(j, _):
        at = pl.multiple_of(j * 2 * LEAF_PTS, 2 * LEAF_PTS)
        x = values[:, pl.ds(at, 2 * LEAF_PTS)]
        v = basis[:, pl.ds(at, 2 * LEAF_PTS)]
        out = times_t(
            jnp.concatenate([x[:, :LEAF_PTS], x[:, LEAF_PTS:]], axis=0),
            jnp.concatenate([v[:, :LEAF_PTS], v[:, LEAF_PTS:]], axis=0),
        )
        pair = join(out)
        pairs[j] = pair
        widen(0, RIMS[0] + 2 * j, pair, 2)
        return 0

    lax.fori_loop(0, LEAVES_DEV // 2, leaf_pair, 0, unroll=4)
    send_rim(0)
    loads[3].wait()
    for h in range(1, LOC_LEVELS):

        def node_pair(j, _, h=h):
            below = pairs[pl.ds(PAIR_AT[h - 1] + 2 * j, 2)].reshape(2 * RHS, 2 * RANK)
            weights = transfer[pl.ds(TRANSFER_AT[h] + 2 * j, 2)].reshape(2 * RANK, 2 * RANK)
            pair = join(times_t(below, weights))
            pairs[PAIR_AT[h] + j] = pair
            widen(h, RIMS[h] + 2 * j, pair, 2)
            return 0

        total = COUNTS[h] // 2
        lax.fori_loop(0, total, node_pair, 0, unroll=min(4, total))
        send_rim(h)
    root = transfer[LEAVES_DEV - 2]
    root_twice = jnp.concatenate([root, root], axis=0)
    current = times_t(pairs[PAIR_AT[LOC_LEVELS - 1]], root_twice)

    loads[5].wait()
    loads[6].wait()
    half = (lax.broadcasted_iota(jnp.int32, (RHS, 2 * RANK), 1) >= RANK).astype(jnp.int32)
    top_field = []
    for r, (base, bits) in enumerate(rounds):
        packed[r] = jnp.where(lane_high[: RHS // 2], current[RHS // 2 :], current[: RHS // 2])
        copies = []
        for k in range(1, 1 << bits):
            copy = pltpu.make_async_remote_copy(
                src_ref=packed.at[r],
                dst_ref=gathered.at[r, k],
                send_sem=top_send.at[r, k],
                recv_sem=top_recv.at[r, k],
                device_id=(me ^ (k << base),),
                device_id_type=MESH,
            )
            copy.start()
            copies.append(copy)
        for copy in copies:
            copy.wait()
        nodes = [current]
        for k in range(1, 1 << bits):
            got = gathered[r, k]
            turned = pltpu.roll(got, RANK, 1)
            low = lane_high[: RHS // 2]
            nodes.append(
                jnp.concatenate(
                    [jnp.where(low, turned, got), jnp.where(low, got, turned)], axis=0
                )
            )
        for step in range(base, base + bits):
            own_half = half == ((me >> step) & 1)
            block = top_coupling[step]
            top_field.append(
                times_t(
                    jnp.where(own_half, nodes[1], 0.0), jnp.concatenate([block, block], axis=0)
                )
            )
            if step + 1 < levels_top:
                is_left = half == ((me >> step) & 1)
                joined = [
                    jnp.where(is_left, nodes[2 * j], nodes[2 * j + 1])
                    for j in range(len(nodes) // 2)
                ]
                weights = top_transfer[step]
                out = times_t(
                    jnp.concatenate(joined, axis=0), jnp.concatenate([weights, weights], axis=0)
                )
                nodes = [out[RHS * j : RHS * (j + 1)] for j in range(len(joined))]
                current = nodes[0]

    loads[4].wait()
    for h in range(LOC_LEVELS):
        for copy in rim_copies[h]:
            copy.wait()
        if RIMS[h] == 1:
            widen(h, 0, rim[0, RIM_AT[h]], 1)
            widen(h, 1 + COUNTS[h], rim[1, RIM_AT[h]], 0)
        else:
            for n in range(RIM_PAIRS[h]):
                widen(h, 2 * n, rim[0, RIM_AT[h] + n], 2)
                widen(h, RIMS[h] + COUNTS[h] + 2 * n, rim[1, RIM_AT[h] + n], 2)

        def couple(j, _, h=h):
            start = RIMS[h] - me * COUNTS[h]
            last = COUNTS[h] + 2 * RIMS[h] - 1
            rows = []
            for n in range(2):
                k = COUPLING_AT[h] + 2 * j + n
                first = wide[WIDE_AT[h] + jnp.clip(partners[k, 0] + start, 0, last)]
                second = wide[WIDE_AT[h] + jnp.clip(partners[k, 1] + start, 0, last)]
                rows.append(jnp.where(lane_high, second, first))
            weights = coupling[pl.ds(COUPLING_AT[h] + 2 * j, 2)].reshape(2 * RANK, 2 * RANK)
            field[PAIR_AT[h] + j] = join(times_t(jnp.concatenate(rows, axis=0), weights))
            return 0

        total = COUNTS[h] // 2
        lax.fori_loop(0, total, couple, 0, unroll=min(4, total))

    spread = jnp.where(half == 0, top_field[-1], 0.0)
    for step in reversed(range(levels_top - 1)):
        weights = top_transfer[step]
        out = times(spread, jnp.concatenate([weights, weights], axis=0))
        spread = jnp.where(half == ((me >> step) & 1), out + top_field[step], 0.0)
    out = times(spread, root_twice)
    down[PAIR_AT[LOC_LEVELS - 1]] = out + field[PAIR_AT[LOC_LEVELS - 1]]

    def apart(pair):
        return jnp.concatenate(
            [jnp.where(lane_high, 0.0, pair), jnp.where(lane_high, pair, 0.0)], axis=0
        )

    for h in range(LOC_LEVELS - 1, 0, -1):

        def descend(j, _, h=h):
            weights = transfer[pl.ds(TRANSFER_AT[h] + 2 * j, 2)].reshape(2 * RANK, 2 * RANK)
            out = times(apart(down[PAIR_AT[h] + j]), weights)
            below = PAIR_AT[h - 1] + 2 * j
            down[below] = out[:RHS] + field[below]
            down[below + 1] = out[RHS:] + field[below + 1]
            return 0

        total = COUNTS[h] // 2
        lax.fori_loop(0, total, descend, 0, unroll=min(4, total))

    def expand(j, _):
        at = pl.multiple_of(j * 2 * LEAF_PTS, 2 * LEAF_PTS)
        v = basis[:, pl.ds(at, 2 * LEAF_PTS)]
        out = times(
            apart(down[j]), jnp.concatenate([v[:, :LEAF_PTS], v[:, LEAF_PTS:]], axis=0)
        )
        far[:, pl.ds(at, 2 * LEAF_PTS)] = jnp.concatenate([out[:RHS], out[RHS:]], axis=1)
        return 0

    lax.fori_loop(0, LEAVES_DEV // 2, expand, 0, unroll=4)
    for copy in face_copies:
        copy.wait()


def tree(devices, values, points, basis, transfer, coupling, top_transfer, top_coupling, partners):
    leaf_points = LEAVES_DEV * LEAF_PTS
    rounds = rounds_of(devices)
    width = 1 << ROUND_BITS
    vmem = pl.BlockSpec(memory_space=pltpu.VMEM)
    return pl.pallas_call(
        functools.partial(tree_kernel, devices),
        out_shape=[
            jax.ShapeDtypeStruct((RHS, leaf_points), f32),
            jax.ShapeDtypeStruct((2, FACE, RHS, LEAF_PTS), f32),
            jax.ShapeDtypeStruct((2, 3, FACE, LEAF_PTS), f32),
        ],
        in_specs=[pl.BlockSpec(memory_space=pl.ANY)] * 7
        + [pl.BlockSpec(memory_space=pltpu.SMEM)],
        out_specs=[vmem] * 3,
        scratch_shapes=[
            pltpu.VMEM((RHS, leaf_points), f32),
            pltpu.VMEM((3, leaf_points), f32),
            pltpu.VMEM((RANK, leaf_points), f32),
            pltpu.VMEM(transfer.shape, f32),
            pltpu.VMEM(coupling.shape, f32),
            pltpu.VMEM(top_transfer.shape, f32),
            pltpu.VMEM(top_coupling.shape, f32),
            pltpu.VMEM((2, FACE, RHS, LEAF_PTS), f32),
            pltpu.VMEM((2, 3, FACE, LEAF_PTS), f32),
            pltpu.VMEM((LEAVES_DEV - 1, RHS, 2 * RANK), f32),
            pltpu.VMEM((2, sum(RIM_PAIRS), RHS, 2 * RANK), f32),
            pltpu.VMEM((WIDE_AT[-1], RHS, 2 * RANK), f32),
            pltpu.VMEM((LEAVES_DEV - 1, RHS, 2 * RANK), f32),
            pltpu.VMEM((LEAVES_DEV - 1, RHS, 2 * RANK), f32),
            pltpu.VMEM((len(rounds), RHS // 2, 2 * RANK), f32),
            pltpu.VMEM((len(rounds), width, RHS // 2, 2 * RANK), f32),
            pltpu.SemaphoreType.DMA((7,)),
            pltpu.SemaphoreType.DMA((2, 2)),
            pltpu.SemaphoreType.DMA((2, 2)),
            pltpu.SemaphoreType.DMA((2, LOC_LEVELS)),
            pltpu.SemaphoreType.DMA((2, LOC_LEVELS)),
            pltpu.SemaphoreType.DMA((len(rounds), width)),
            pltpu.SemaphoreType.DMA((len(rounds), width)),
        ],
        compiler_params=pltpu.CompilerParams(
            collective_id=0, has_side_effects=True, vmem_limit_bytes=40 << 20
        ),
        name="tree",
    )(values, points, basis, transfer, coupling, top_transfer, top_coupling, partners)


def near_kernel(
    columns,
    counts,
    values,
    points,
    halo_x,
    halo_p,
    far,
    out,
    rows_t,
    rows_s,
    target,
    source,
    rhs,
    total,
):
    me = lax.axis_index("leaf")
    leaf_points = LEAVES_DEV * LEAF_PTS

    def three(a):
        high = a.astype(bf16).astype(f32)
        rest = a - high
        mid = rest.astype(bf16).astype(f32)
        return high, mid, rest - mid

    def lay(at, width, coords, with_target):
        lanes = pl.ds(at, width)
        square = coords[0] * coords[0] + coords[1] * coords[1] + coords[2] * coords[2]
        norm = three(square)
        ones = jnp.ones_like(square)
        for axis in range(3):
            high, mid, low = three(coords[axis])
            for n, part in enumerate((high, high, mid, high, low, mid)):
                rows_s[3 * n + axis : 3 * n + axis + 1, lanes] = part
            rows_s[18 + axis : 19 + axis, lanes] = norm[axis]
            rows_s[21 + axis : 22 + axis, lanes] = ones
            if with_target:
                for n, part in enumerate((high, mid, high, low, high, mid)):
                    rows_t[3 * n + axis : 3 * n + axis + 1, lanes] = -2.0 * part
                rows_t[18 + axis : 19 + axis, lanes] = ones
                rows_t[21 + axis : 22 + axis, lanes] = norm[axis]

    corner = (me * 4 + 2).astype(f32)
    centre = (corner, 2.0, 2.0)
    rows_s[24:32, :] = jnp.zeros((8, SOURCES * LEAF_PTS), f32)
    rows_t[24:32, :] = jnp.zeros((8, leaf_points), f32)
    lay(
        0,
        leaf_points,
        [(points[axis : axis + 1, :] - centre[axis]) * SCALE for axis in range(3)],
        True,
    )
    for side in range(2):
        for e in range(FACE):
            lay(
                leaf_points + (side * FACE + e) * LEAF_PTS,
                LEAF_PTS,
                [
                    (halo_p[side, axis, e : e + 1, :] - centre[axis]) * SCALE
                    for axis in range(3)
                ],
                False,
            )

    def prepare(n, _):
        at = pl.multiple_of(n * LEAF_PTS, LEAF_PTS)
        lanes = pl.ds(at, LEAF_PTS)
        target[n] = rows_t[:, lanes].astype(bf16)
        source[n] = rows_s[:, lanes].T.astype(bf16)
        high, low = halves(values[:, lanes])
        rhs[n, :RHS] = high
        rhs[n, RHS:] = low
        total[n] = jnp.zeros((RHS, LEAF_PTS), f32)
        return 0

    lax.fori_loop(0, LEAVES_DEV, prepare, 0, unroll=4)

    def prepare_halo(n, _):
        for side in range(2):
            at = pl.multiple_of((LEAVES_DEV + side * FACE + n) * LEAF_PTS, LEAF_PTS)
            slot = LEAVES_DEV + side * FACE + n
            source[slot] = rows_s[:, pl.ds(at, LEAF_PTS)].T.astype(bf16)
            high, low = halves(halo_x[side, n])
            rhs[slot, :RHS] = high
            rhs[slot, RHS:] = low
        return 0

    lax.fori_loop(0, FACE, prepare_halo, 0, unroll=2)
    target[LEAVES_DEV] = jnp.zeros((32, LEAF_PTS), bf16)

    live = lax.fori_loop(0, LEAVES_DEV, lambda n, s: s + counts[n], 0)

    def group(_, state):
        leaf, slot = state
        work = []
        for _ in range(BLOCKS):
            inside = jnp.minimum(leaf, LEAVES_DEV - 1)
            column = columns[inside, slot] - me * LEAVES_DEV
            inner = column & (LEAVES_DEV - 1)
            face = ((inner >> 1) & 3) | (((inner >> 4) & 3) << 2)
            beyond = jnp.where(column < 0, LEAVES_DEV + face, LEAVES_DEV + FACE + face)
            work.append((leaf, jnp.where((column >= 0) & (column < LEAVES_DEV), column, beyond)))
            more = slot + 1 < counts[inside]
            slot = jnp.where(more, slot + 1, 0)
            leaf = jnp.minimum(jnp.where(more, leaf, leaf + 1), LEAVES_DEV)
        for n, q in work:
            square = jnp.dot(source[q], target[n], preferred_element_type=f32)
            square = jnp.maximum(square, 1e-12)
            t = square * lax.rsqrt(square)
            high, low = halves((t + LOG2E) * jnp.exp2(-t))
            x = rhs[q]
            both = jnp.dot(x, high, preferred_element_type=f32)
            rest = jnp.dot(x[:RHS], low, preferred_element_type=f32)
            total[n] = total[n] + (both[:RHS] + (both[RHS:] + rest))
        return leaf, slot

    lax.fori_loop(0, (live + BLOCKS - 1) // BLOCKS, group, (jnp.int32(0), jnp.int32(0)))

    def finish(n, _):
        lanes = pl.ds(pl.multiple_of(n * LEAF_PTS, LEAF_PTS), LEAF_PTS)
        out[:, lanes] = far[:, lanes] + AMPLITUDE * total[n]
        return 0

    lax.fori_loop(0, LEAVES_DEV, finish, 0, unroll=4)


def near(columns, counts, values, points, halo_x, halo_p, far):
    leaf_points = LEAVES_DEV * LEAF_PTS
    vmem = pl.BlockSpec(memory_space=pltpu.VMEM)
    smem = pl.BlockSpec(memory_space=pltpu.SMEM)
    return pl.pallas_call(
        near_kernel,
        out_shape=jax.ShapeDtypeStruct((RHS, leaf_points), f32),
        in_specs=[smem, smem] + [vmem] * 5,
        out_specs=vmem,
        scratch_shapes=[
            pltpu.VMEM((32, leaf_points), f32),
            pltpu.VMEM((32, SOURCES * LEAF_PTS), f32),
            pltpu.VMEM((LEAVES_DEV + 1, 32, LEAF_PTS), bf16),
            pltpu.VMEM((SOURCES, LEAF_PTS, 32), bf16),
            pltpu.VMEM((SOURCES, 2 * RHS, LEAF_PTS), bf16),
            pltpu.VMEM((LEAVES_DEV + 1, RHS, LEAF_PTS), f32),
        ],
        compiler_params=pltpu.CompilerParams(vmem_limit_bytes=40 << 20),
        name="near",
    )(columns, counts, values, points, halo_x, halo_p, far)


def local(
    values,
    points,
    basis,
    local_transfer,
    local_coupling,
    local_partners,
    top_transfer,
    top_coupling,
    near_cols,
    near_count,
):
    devices = lax.axis_size("leaf")
    far, halo_x, halo_p = tree(
        devices,
        values,
        points,
        basis,
        local_transfer,
        local_coupling,
        top_transfer,
        top_coupling,
        local_partners,
    )
    return near(near_cols, near_count, values, points, halo_x, halo_p, far)


def solution(mesh):
    placed = (
        P(None, "leaf"),
        P(None, "leaf"),
        P(None, "leaf"),
        P("leaf", None, None),
        P("leaf", None, None),
        P("leaf", None),
        P(),
        P(),
        P("leaf", None),
        P("leaf"),
    )
    return jax.shard_map(
        local, mesh=mesh, in_specs=placed, out_specs=P(None, "leaf"), check_vma=False
    )
```

```python
import functools
import math

import jax
import jax.numpy as jnp
import numpy as np
from jax import lax
from jax.experimental import pallas as pl
from jax.experimental.pallas import tpu as pltpu
from jax.sharding import PartitionSpec as P

LEAF_PTS = 128
RANK = 64
RHS = 32
NEAR_SLOTS = 8
COUPLE = 2
WINDOW = 4
LOC_LEVELS = 6
LEAVES_DEV = 64
FACE = 16
SOURCES = LEAVES_DEV + 2 * FACE
ROUND_BITS = 4
BLOCKS = 8
UNROLL = 8

MESH = pl.DeviceIdType.MESH
bf16 = jnp.bfloat16
f32 = jnp.float32
LOG2E = 1.4426950408889634
SCALE = math.sqrt(3.0) / 0.5 * LOG2E
AMPLITUDE = 0.25 / LOG2E

COUNTS = [LEAVES_DEV >> h for h in range(LOC_LEVELS + 1)]
RIMS = [min(WINDOW, (LEAVES_DEV >> h) // 2) for h in range(LOC_LEVELS)]
PAIR_AT = [LEAVES_DEV - COUNTS[h] for h in range(LOC_LEVELS)]
RIM_PAIRS = [max(1, r // 2) for r in RIMS]
RIM_AT = [sum(RIM_PAIRS[:h]) for h in range(LOC_LEVELS)]
WIDE_AT = [sum(COUNTS[g] + 2 * RIMS[g] for g in range(h)) for h in range(LOC_LEVELS + 1)]
TRANSFER_AT = [LEAVES_DEV - 2 * c for c in COUNTS]
COUPLING_AT = [2 * LEAVES_DEV - 2 * c for c in COUNTS]


def rounds_of(devices):
    total = devices.bit_length() - 1
    return [(b, min(ROUND_BITS, total - b)) for b in range(0, total, ROUND_BITS)]


def halves(a):
    high = a.astype(bf16)
    return high, (a - high.astype(f32)).astype(bf16)


def doubled(left):
    high, low = halves(left)
    return jnp.concatenate(
        [
            jnp.concatenate([high, high], axis=1),
            jnp.concatenate([low, jnp.zeros_like(low)], axis=1),
        ],
        axis=0,
    )


def apply(left, stacked):
    rows = left.shape[0]
    out = jnp.dot(doubled(left), stacked, preferred_element_type=f32)
    return out[:rows] + out[rows:]


def times(left, right):
    return apply(left, jnp.concatenate(halves(right), axis=0))


def times_t(left, right):
    rows = left.shape[0]
    out = lax.dot_general(
        doubled(left),
        jnp.concatenate(halves(right), axis=1),
        (((1,), (1,)), ((), ())),
        preferred_element_type=f32,
    )
    return out[:rows] + out[rows:]


def face_leaf(side, e):
    spread = ((e & 3) << 1) | ((e >> 2) << 4)
    return spread + 9 * side


def tree_kernel(
    devices,
    values_h,
    points_h,
    basis_h,
    transfer_h,
    coupling_h,
    top_transfer_h,
    top_coupling_h,
    partners,
    far,
    halo_x,
    halo_p,
    values,
    points,
    basis,
    transfer,
    coupling,
    top_transfer,
    top_coupling,
    face_x,
    face_p,
    pairs,
    rim,
    wide,
    field,
    down,
    packed,
    gathered,
    top_up_w,
    top_down_w,
    top_field_w,
    load_sem,
    face_send,
    face_recv,
    rim_ssem,
    rim_rsem,
    top_send,
    top_recv,
):
    me = lax.axis_index("leaf")
    right = lax.rem(me + 1, devices)
    left = lax.rem(me + devices - 1, devices)
    rounds = rounds_of(devices)
    levels_top = devices.bit_length() - 1

    barrier = pltpu.get_barrier_semaphore()
    greeted = 0
    for other in (left, right):
        pl.semaphore_signal(barrier, inc=1, device_id=(other,), device_id_type=MESH)
        greeted += 1
    for base, bits in rounds:
        for k in range(1, 1 << bits):
            pl.semaphore_signal(
                barrier, inc=1, device_id=(me ^ (k << base),), device_id_type=MESH
            )
            greeted += 1

    loads = {}
    for n, (name, src, dst) in enumerate(
        [
            ("top_transfer", top_transfer_h, top_transfer),
            ("top_coupling", top_coupling_h, top_coupling),
            ("values", values_h, values),
            ("basis", basis_h, basis),
            ("points", points_h, points),
            ("transfer", transfer_h, transfer),
            ("coupling", coupling_h, coupling),
        ]
    ):
        loads[name] = pltpu.make_async_copy(src, dst, load_sem.at[n])
        loads[name].start()

    lane_high = lax.broadcasted_iota(jnp.int32, (RHS, 2 * RANK), 1) >= RANK

    def join(out):
        return jnp.where(lane_high, out[RHS:], out[:RHS])

    def store_split(ref, at, matrix):
        high, low = halves(matrix)
        ref[at, : 2 * RANK] = high
        ref[at, 2 * RANK :] = low

    loads["top_transfer"].wait()
    loads["top_coupling"].wait()
    for step in range(levels_top):
        block = top_coupling[step]
        store_split(top_field_w, step, jnp.concatenate([block, block], axis=0).T)
        if step + 1 < levels_top:
            block = top_transfer[step]
            twice = jnp.concatenate([block, block], axis=0)
            store_split(top_up_w, step, twice.T)
            store_split(top_down_w, step, twice)

    rim_copies = [[] for _ in range(LOC_LEVELS)]

    def send_rim(h):
        count = RIM_PAIRS[h]
        at = RIM_AT[h]
        first = PAIR_AT[h]
        last = first + COUNTS[h] // 2 - count
        for side, (other, start) in enumerate(((right, last), (left, first))):
            copy = pltpu.make_async_remote_copy(
                src_ref=pairs.at[pl.ds(start, count)],
                dst_ref=rim.at[side, pl.ds(at, count)],
                send_sem=rim_ssem.at[side, h],
                recv_sem=rim_rsem.at[side, h],
                device_id=(other,),
                device_id_type=MESH,
            )
            copy.start()
            rim_copies[h].append(copy)

    def widen(h, slot, pair, which):
        turned = pltpu.roll(pair, RANK, 1)
        if which != 1:
            wide[WIDE_AT[h] + slot] = jnp.where(lane_high, turned, pair)
        if which != 0:
            wide[WIDE_AT[h] + slot + (which == 2)] = jnp.where(lane_high, pair, turned)

    loads["values"].wait()
    loads["basis"].wait()

    def leaf_pair(j, _):
        at = pl.multiple_of(j * 2 * LEAF_PTS, 2 * LEAF_PTS)
        x = values[:, pl.ds(at, 2 * LEAF_PTS)]
        v = basis[:, pl.ds(at, 2 * LEAF_PTS)]
        out = times_t(
            jnp.concatenate([x[:, :LEAF_PTS], x[:, LEAF_PTS:]], axis=0),
            jnp.concatenate([v[:, :LEAF_PTS], v[:, LEAF_PTS:]], axis=0),
        )
        pair = join(out)
        pairs[j] = pair
        widen(0, RIMS[0] + 2 * j, pair, 2)
        return 0

    lax.fori_loop(0, LEAVES_DEV // 2, leaf_pair, 0, unroll=UNROLL)
    loads["points"].wait()
    for side in range(2):
        for e in range(FACE):
            leaf = face_leaf(1 - side, e)
            at = leaf * LEAF_PTS
            face_x[side, e] = values[:, at : at + LEAF_PTS]
            for axis in range(3):
                face_p[side, axis, e : e + 1, :] = points[axis : axis + 1, at : at + LEAF_PTS]
    pl.semaphore_wait(barrier, greeted)
    face_copies = []
    for side, other in ((0, right), (1, left)):
        for n, (src, dst) in enumerate(((face_x, halo_x), (face_p, halo_p))):
            copy = pltpu.make_async_remote_copy(
                src_ref=src.at[side],
                dst_ref=dst.at[side],
                send_sem=face_send.at[side, n],
                recv_sem=face_recv.at[side, n],
                device_id=(other,),
                device_id_type=MESH,
            )
            copy.start()
            face_copies.append(copy)

    send_rim(0)
    loads["transfer"].wait()
    for h in range(1, LOC_LEVELS):

        def node_pair(j, _, h=h):
            below = pairs[pl.ds(PAIR_AT[h - 1] + 2 * j, 2)].reshape(2 * RHS, 2 * RANK)
            weights = transfer[pl.ds(TRANSFER_AT[h] + 2 * j, 2)].reshape(2 * RANK, 2 * RANK)
            pair = join(times_t(below, weights))
            pairs[PAIR_AT[h] + j] = pair
            widen(h, RIMS[h] + 2 * j, pair, 2)
            return 0

        total = COUNTS[h] // 2
        lax.fori_loop(0, total, node_pair, 0, unroll=min(UNROLL, total))
        send_rim(h)
    root = transfer[LEAVES_DEV - 2]
    root_twice = jnp.concatenate([root, root], axis=0)
    current = times_t(pairs[PAIR_AT[LOC_LEVELS - 1]], root_twice)

    def couple_level(h):
        for copy in rim_copies[h]:
            copy.wait()
        if RIMS[h] == 1:
            widen(h, 0, rim[0, RIM_AT[h]], 1)
            widen(h, 1 + COUNTS[h], rim[1, RIM_AT[h]], 0)
        else:
            for n in range(RIM_PAIRS[h]):
                widen(h, 2 * n, rim[0, RIM_AT[h] + n], 2)
                widen(h, RIMS[h] + COUNTS[h] + 2 * n, rim[1, RIM_AT[h] + n], 2)

        def couple(j, _, h=h):
            start = RIMS[h] - me * COUNTS[h]
            last = COUNTS[h] + 2 * RIMS[h] - 1
            rows = []
            for n in range(2):
                k = COUPLING_AT[h] + 2 * j + n
                first = wide[WIDE_AT[h] + jnp.clip(partners[0, k] + start, 0, last)]
                second = wide[WIDE_AT[h] + jnp.clip(partners[1, k] + start, 0, last)]
                rows.append(jnp.where(lane_high, second, first))
            weights = coupling[pl.ds(COUPLING_AT[h] + 2 * j, 2)].reshape(2 * RANK, 2 * RANK)
            field[PAIR_AT[h] + j] = join(times_t(jnp.concatenate(rows, axis=0), weights))
            return 0

        total = COUNTS[h] // 2
        lax.fori_loop(0, total, couple, 0, unroll=min(UNROLL, total))

    half = (lax.broadcasted_iota(jnp.int32, (RHS, 2 * RANK), 1) >= RANK).astype(jnp.int32)
    top_field = []
    for r, (base, bits) in enumerate(rounds):
        packed[r] = jnp.where(lane_high[: RHS // 2], current[RHS // 2 :], current[: RHS // 2])
        copies = []
        for k in range(1, 1 << bits):
            copy = pltpu.make_async_remote_copy(
                src_ref=packed.at[r],
                dst_ref=gathered.at[r, k],
                send_sem=top_send.at[r, k],
                recv_sem=top_recv.at[r, k],
                device_id=(me ^ (k << base),),
                device_id_type=MESH,
            )
            copy.start()
            copies.append(copy)
        if r == 0:
            loads["coupling"].wait()
            couple_level(0)
        if r == len(rounds) - 1:
            for h in range(1, LOC_LEVELS):
                couple_level(h)
        for copy in copies:
            copy.wait()
        nodes = [current]
        for k in range(1, 1 << bits):
            got = gathered[r, k]
            turned = pltpu.roll(got, RANK, 1)
            low = lane_high[: RHS // 2]
            nodes.append(
                jnp.concatenate(
                    [jnp.where(low, turned, got), jnp.where(low, got, turned)], axis=0
                )
            )
        for step in range(base, base + bits):
            own_half = half == ((me >> step) & 1)
            top_field.append(apply(jnp.where(own_half, nodes[1], 0.0), top_field_w[step]))
            if step + 1 < levels_top:
                is_left = half == ((me >> step) & 1)
                joined = [
                    jnp.where(is_left, nodes[2 * j], nodes[2 * j + 1])
                    for j in range(len(nodes) // 2)
                ]
                out = apply(jnp.concatenate(joined, axis=0), top_up_w[step])
                nodes = [out[RHS * j : RHS * (j + 1)] for j in range(len(joined))]
                current = nodes[0]

    spread = jnp.where(half == 0, top_field[-1], 0.0)
    for step in reversed(range(levels_top - 1)):
        out = apply(spread, top_down_w[step])
        spread = jnp.where(half == ((me >> step) & 1), out + top_field[step], 0.0)
    out = times(spread, root_twice)
    down[PAIR_AT[LOC_LEVELS - 1]] = out + field[PAIR_AT[LOC_LEVELS - 1]]

    def apart(pair):
        return jnp.concatenate(
            [jnp.where(lane_high, 0.0, pair), jnp.where(lane_high, pair, 0.0)], axis=0
        )

    for h in range(LOC_LEVELS - 1, 0, -1):

        def descend(j, _, h=h):
            weights = transfer[pl.ds(TRANSFER_AT[h] + 2 * j, 2)].reshape(2 * RANK, 2 * RANK)
            out = times(apart(down[PAIR_AT[h] + j]), weights)
            below = PAIR_AT[h - 1] + 2 * j
            down[below] = out[:RHS] + field[below]
            down[below + 1] = out[RHS:] + field[below + 1]
            return 0

        total = COUNTS[h] // 2
        lax.fori_loop(0, total, descend, 0, unroll=min(UNROLL, total))

    def expand(j, _):
        at = pl.multiple_of(j * 2 * LEAF_PTS, 2 * LEAF_PTS)
        v = basis[:, pl.ds(at, 2 * LEAF_PTS)]
        out = times(
            apart(down[j]), jnp.concatenate([v[:, :LEAF_PTS], v[:, LEAF_PTS:]], axis=0)
        )
        far[:, pl.ds(at, 2 * LEAF_PTS)] = jnp.concatenate([out[:RHS], out[RHS:]], axis=1)
        return 0

    lax.fori_loop(0, LEAVES_DEV // 2, expand, 0, unroll=UNROLL)
    for copy in face_copies:
        copy.wait()


def tree(devices, values, points, basis, transfer, coupling, top_transfer, top_coupling, partners):
    leaf_points = LEAVES_DEV * LEAF_PTS
    rounds = rounds_of(devices)
    width = 1 << ROUND_BITS
    vmem = pl.BlockSpec(memory_space=pltpu.VMEM)
    return pl.pallas_call(
        functools.partial(tree_kernel, devices),
        out_shape=[
            jax.ShapeDtypeStruct((RHS, leaf_points), f32),
            jax.ShapeDtypeStruct((2, FACE, RHS, LEAF_PTS), f32),
            jax.ShapeDtypeStruct((2, 3, FACE, LEAF_PTS), f32),
        ],
        in_specs=[pl.BlockSpec(memory_space=pl.ANY)] * 7
        + [pl.BlockSpec(memory_space=pltpu.SMEM)],
        out_specs=[vmem] * 3,
        scratch_shapes=[
            pltpu.VMEM((RHS, leaf_points), f32),
            pltpu.VMEM((3, leaf_points), f32),
            pltpu.VMEM((RANK, leaf_points), f32),
            pltpu.VMEM(transfer.shape, f32),
            pltpu.VMEM(coupling.shape, f32),
            pltpu.VMEM(top_transfer.shape, f32),
            pltpu.VMEM(top_coupling.shape, f32),
            pltpu.VMEM((2, FACE, RHS, LEAF_PTS), f32),
            pltpu.VMEM((2, 3, FACE, LEAF_PTS), f32),
            pltpu.VMEM((LEAVES_DEV - 1, RHS, 2 * RANK), f32),
            pltpu.VMEM((2, sum(RIM_PAIRS), RHS, 2 * RANK), f32),
            pltpu.VMEM((WIDE_AT[-1], RHS, 2 * RANK), f32),
            pltpu.VMEM((LEAVES_DEV - 1, RHS, 2 * RANK), f32),
            pltpu.VMEM((LEAVES_DEV - 1, RHS, 2 * RANK), f32),
            pltpu.VMEM((len(rounds), RHS // 2, 2 * RANK), f32),
            pltpu.VMEM((len(rounds), width, RHS // 2, 2 * RANK), f32),
            pltpu.VMEM((top_transfer.shape[0], 4 * RANK, 2 * RANK), bf16),
            pltpu.VMEM((top_transfer.shape[0], 4 * RANK, 2 * RANK), bf16),
            pltpu.VMEM((top_coupling.shape[0], 4 * RANK, 2 * RANK), bf16),
            pltpu.SemaphoreType.DMA((7,)),
            pltpu.SemaphoreType.DMA((2, 2)),
            pltpu.SemaphoreType.DMA((2, 2)),
            pltpu.SemaphoreType.DMA((2, LOC_LEVELS)),
            pltpu.SemaphoreType.DMA((2, LOC_LEVELS)),
            pltpu.SemaphoreType.DMA((len(rounds), width)),
            pltpu.SemaphoreType.DMA((len(rounds), width)),
        ],
        compiler_params=pltpu.CompilerParams(
            collective_id=0, has_side_effects=True, vmem_limit_bytes=60 << 20
        ),
        name="tree",
    )(values, points, basis, transfer, coupling, top_transfer, top_coupling, partners)


def near_kernel(
    columns,
    counts,
    values,
    points,
    halo_x,
    halo_p,
    far,
    out,
    rows_t,
    rows_s,
    target,
    source,
    rhs,
    total,
    squares,
    kernels,
    queue,
):
    me = lax.axis_index("leaf")
    leaf_points = LEAVES_DEV * LEAF_PTS

    def three(a):
        high = a.astype(bf16).astype(f32)
        rest = a - high
        mid = rest.astype(bf16).astype(f32)
        return high, mid, rest - mid

    def lay(at, width, coords, with_target):
        lanes = pl.ds(at, width)
        square = coords[0] * coords[0] + coords[1] * coords[1] + coords[2] * coords[2]
        norm = three(square)
        ones = jnp.ones_like(square)
        for axis in range(3):
            high, mid, low = three(coords[axis])
            for n, part in enumerate((high, high, mid, high, low, mid)):
                rows_s[3 * n + axis : 3 * n + axis + 1, lanes] = part
            rows_s[18 + axis : 19 + axis, lanes] = norm[axis]
            rows_s[21 + axis : 22 + axis, lanes] = ones
            if with_target:
                for n, part in enumerate((high, mid, high, low, high, mid)):
                    rows_t[3 * n + axis : 3 * n + axis + 1, lanes] = -2.0 * part
                rows_t[18 + axis : 19 + axis, lanes] = ones
                rows_t[21 + axis : 22 + axis, lanes] = norm[axis]

    corner = (me * 4 + 2).astype(f32)
    centre = (corner, 2.0, 2.0)
    rows_s[24:32, :] = jnp.zeros((8, SOURCES * LEAF_PTS), f32)
    rows_t[24:32, :] = jnp.zeros((8, leaf_points), f32)
    lay(
        0,
        leaf_points,
        [(points[axis : axis + 1, :] - centre[axis]) * SCALE for axis in range(3)],
        True,
    )
    for side in range(2):
        for e in range(FACE):
            lay(
                leaf_points + (side * FACE + e) * LEAF_PTS,
                LEAF_PTS,
                [
                    (halo_p[side, axis, e : e + 1, :] - centre[axis]) * SCALE
                    for axis in range(3)
                ],
                False,
            )

    def lay_rhs(n, high, low):
        rhs[n, :RHS, :LEAF_PTS] = high
        rhs[n, :RHS, LEAF_PTS:] = high
        rhs[n, RHS:, :LEAF_PTS] = low
        rhs[n, RHS:, LEAF_PTS:] = jnp.zeros_like(low)

    def prepare(n, _):
        at = pl.multiple_of(n * LEAF_PTS, LEAF_PTS)
        lanes = pl.ds(at, LEAF_PTS)
        target[n] = rows_t[:, lanes].astype(bf16)
        source[n] = rows_s[:, lanes].T.astype(bf16)
        high, low = halves(values[:, lanes])
        lay_rhs(n, high, low)
        total[n] = jnp.zeros((RHS, LEAF_PTS), f32)
        return 0

    lax.fori_loop(0, LEAVES_DEV, prepare, 0, unroll=4)

    def prepare_halo(n, _):
        for side in range(2):
            at = pl.multiple_of((LEAVES_DEV + side * FACE + n) * LEAF_PTS, LEAF_PTS)
            slot = LEAVES_DEV + side * FACE + n
            source[slot] = rows_s[:, pl.ds(at, LEAF_PTS)].T.astype(bf16)
            high, low = halves(halo_x[side, n])
            lay_rhs(slot, high, low)
        return 0

    lax.fori_loop(0, FACE, prepare_halo, 0, unroll=2)
    target[LEAVES_DEV] = jnp.zeros((32, LEAF_PTS), bf16)

    live = lax.fori_loop(0, LEAVES_DEV, lambda n, s: s + counts[n], 0, unroll=8)
    for b in range(BLOCKS):
        for stage in range(2):
            queue[stage, b] = LEAVES_DEV
            queue[2 + stage, b] = 0
        squares[b] = jnp.zeros((LEAF_PTS, LEAF_PTS), f32)
        kernels[b] = jnp.zeros((2 * LEAF_PTS, LEAF_PTS), bf16)

    def group(_, state):
        leaf, slot = state
        for b in range(BLOCKS):
            n = queue[1, b]
            out = jnp.dot(rhs[queue[3, b]], kernels[b], preferred_element_type=f32)
            total[n] = total[n] + (out[:RHS] + out[RHS:])
            queue[1, b] = queue[0, b]
            queue[3, b] = queue[2, b]
        for b in range(BLOCKS):
            square = jnp.maximum(squares[b], 1e-12)
            t = square * lax.rsqrt(square)
            high, low = halves((t + LOG2E) * jnp.exp2(-t))
            kernels[b, :LEAF_PTS] = high
            kernels[b, LEAF_PTS:] = low
        for b in range(BLOCKS):
            inside = jnp.minimum(leaf, LEAVES_DEV - 1)
            column = columns[slot, inside] - me * LEAVES_DEV
            inner = column & (LEAVES_DEV - 1)
            face = ((inner >> 1) & 3) | (((inner >> 4) & 3) << 2)
            beyond = jnp.where(column < 0, LEAVES_DEV + face, LEAVES_DEV + FACE + face)
            q = jnp.where((column >= 0) & (column < LEAVES_DEV), column, beyond)
            squares[b] = jnp.dot(source[q], target[leaf], preferred_element_type=f32)
            queue[0, b] = leaf
            queue[2, b] = q
            more = slot + 1 < counts[inside]
            slot = jnp.where(more, slot + 1, 0)
            leaf = jnp.minimum(jnp.where(more, leaf, leaf + 1), LEAVES_DEV)
        return leaf, slot

    groups = (live + BLOCKS - 1) // BLOCKS
    lax.fori_loop(0, groups + 2, group, (jnp.int32(0), jnp.int32(0)))

    def finish(n, _):
        lanes = pl.ds(pl.multiple_of(n * LEAF_PTS, LEAF_PTS), LEAF_PTS)
        out[:, lanes] = far[:, lanes] + AMPLITUDE * total[n]
        return 0

    lax.fori_loop(0, LEAVES_DEV, finish, 0, unroll=4)


def near(columns, counts, values, points, halo_x, halo_p, far):
    leaf_points = LEAVES_DEV * LEAF_PTS
    vmem = pl.BlockSpec(memory_space=pltpu.VMEM)
    smem = pl.BlockSpec(memory_space=pltpu.SMEM)
    return pl.pallas_call(
        near_kernel,
        out_shape=jax.ShapeDtypeStruct((RHS, leaf_points), f32),
        in_specs=[smem, smem] + [vmem] * 5,
        out_specs=vmem,
        scratch_shapes=[
            pltpu.VMEM((32, leaf_points), f32),
            pltpu.VMEM((32, SOURCES * LEAF_PTS), f32),
            pltpu.VMEM((LEAVES_DEV + 1, 32, LEAF_PTS), bf16),
            pltpu.VMEM((SOURCES, LEAF_PTS, 32), bf16),
            pltpu.VMEM((SOURCES, 2 * RHS, 2 * LEAF_PTS), bf16),
            pltpu.VMEM((LEAVES_DEV + 1, RHS, LEAF_PTS), f32),
            pltpu.VMEM((BLOCKS, LEAF_PTS, LEAF_PTS), f32),
            pltpu.VMEM((BLOCKS, 2 * LEAF_PTS, LEAF_PTS), bf16),
            pltpu.SMEM((4, BLOCKS), jnp.int32),
        ],
        compiler_params=pltpu.CompilerParams(vmem_limit_bytes=60 << 20),
        name="near",
    )(columns, counts, values, points, halo_x, halo_p, far)


def local(
    values,
    points,
    basis,
    local_transfer,
    local_coupling,
    local_partners,
    top_transfer,
    top_coupling,
    near_cols,
    near_count,
):
    devices = lax.axis_size("leaf")
    far, halo_x, halo_p = tree(
        devices,
        values,
        points,
        basis,
        local_transfer,
        local_coupling,
        top_transfer,
        top_coupling,
        local_partners.T,
    )
    return near(near_cols.T, near_count, values, points, halo_x, halo_p, far)


def solution(mesh):
    placed = (
        P(None, "leaf"),
        P(None, "leaf"),
        P(None, "leaf"),
        P("leaf", None, None),
        P("leaf", None, None),
        P("leaf", None),
        P(),
        P(),
        P("leaf", None),
        P("leaf"),
    )
    return jax.shard_map(
        local, mesh=mesh, in_specs=placed, out_specs=P(None, "leaf"), check_vma=False
    )
```

```python
import functools
import math

import jax
import jax.numpy as jnp
import numpy as np
from jax import lax
from jax.experimental import pallas as pl
from jax.experimental.pallas import tpu as pltpu
from jax.sharding import PartitionSpec as P

LEAF_PTS = 128
RANK = 64
RHS = 32
NEAR_SLOTS = 8
COUPLE = 2
WINDOW = 4
LOC_LEVELS = 6
LEAVES_DEV = 64
FACE = 16
SOURCES = LEAVES_DEV + 2 * FACE
ROUND_BITS = 4
TERMS = 32
UNROLL = 8

MESH = pl.DeviceIdType.MESH
bf16 = jnp.bfloat16
f32 = jnp.float32
LOG2E = 1.4426950408889634
SCALE = math.sqrt(3.0) / 0.5 * LOG2E
AMPLITUDE = 0.25 / LOG2E

COUNTS = [LEAVES_DEV >> h for h in range(LOC_LEVELS + 1)]
RIMS = [min(WINDOW, (LEAVES_DEV >> h) // 2) for h in range(LOC_LEVELS)]
PAIR_AT = [LEAVES_DEV - COUNTS[h] for h in range(LOC_LEVELS)]
RIM_PAIRS = [max(1, r // 2) for r in RIMS]
RIM_AT = [sum(RIM_PAIRS[:h]) for h in range(LOC_LEVELS)]
WIDE_AT = [sum(COUNTS[g] + 2 * RIMS[g] for g in range(h)) for h in range(LOC_LEVELS + 1)]
TRANSFER_AT = [LEAVES_DEV - 2 * c for c in COUNTS]
COUPLING_AT = [2 * LEAVES_DEV - 2 * c for c in COUNTS]


def rounds_of(devices):
    total = devices.bit_length() - 1
    return [(b, min(ROUND_BITS, total - b)) for b in range(0, total, ROUND_BITS)]


def halves(a):
    high = a.astype(bf16)
    return high, (a - high.astype(f32)).astype(bf16)


def doubled(left):
    high, low = halves(left)
    return jnp.concatenate(
        [
            jnp.concatenate([high, high], axis=1),
            jnp.concatenate([low, jnp.zeros_like(low)], axis=1),
        ],
        axis=0,
    )


def apply(left, stacked):
    rows = left.shape[0]
    out = jnp.dot(doubled(left), stacked, preferred_element_type=f32)
    return out[:rows] + out[rows:]


def times(left, right):
    return apply(left, jnp.concatenate(halves(right), axis=0))


def times_t(left, right):
    rows = left.shape[0]
    out = lax.dot_general(
        doubled(left),
        jnp.concatenate(halves(right), axis=1),
        (((1,), (1,)), ((), ())),
        preferred_element_type=f32,
    )
    return out[:rows] + out[rows:]


def face_leaf(side, e):
    spread = ((e & 3) << 1) | ((e >> 2) << 4)
    return spread + 9 * side


def kernel(
    devices,
    values_h,
    points_h,
    basis_h,
    transfer_h,
    coupling_h,
    top_transfer_h,
    top_coupling_h,
    partners,
    columns,
    counts,
    far,
    halo_x,
    halo_p,
    values,
    points,
    basis,
    transfer,
    coupling,
    top_transfer,
    top_coupling,
    face_x,
    face_p,
    pairs,
    rim,
    wide,
    field,
    down,
    packed,
    gathered,
    top_up_w,
    top_down_w,
    top_field_w,
    parts,
    target,
    source_low,
    source_high,
    rhs,
    squares,
    entries_high,
    entries_low,
    load_sem,
    face_send,
    face_recv,
    rim_ssem,
    rim_rsem,
    top_send,
    top_recv,
):
    me = lax.axis_index("leaf")
    right = lax.rem(me + 1, devices)
    left = lax.rem(me + devices - 1, devices)
    rounds = rounds_of(devices)
    levels_top = devices.bit_length() - 1

    barrier = pltpu.get_barrier_semaphore()
    greeted = 0
    for other in (left, right):
        pl.semaphore_signal(barrier, inc=1, device_id=(other,), device_id_type=MESH)
        greeted += 1
    for base, bits in rounds:
        for k in range(1, 1 << bits):
            pl.semaphore_signal(
                barrier, inc=1, device_id=(me ^ (k << base),), device_id_type=MESH
            )
            greeted += 1

    loads = {}
    for n, (name, src, dst) in enumerate(
        [
            ("top_transfer", top_transfer_h, top_transfer),
            ("top_coupling", top_coupling_h, top_coupling),
            ("values", values_h, values),
            ("basis", basis_h, basis),
            ("points", points_h, points),
            ("transfer", transfer_h, transfer),
            ("coupling", coupling_h, coupling),
        ]
    ):
        loads[name] = pltpu.make_async_copy(src, dst, load_sem.at[n])
        loads[name].start()

    lane_high = lax.broadcasted_iota(jnp.int32, (RHS, 2 * RANK), 1) >= RANK

    def join(out):
        return jnp.where(lane_high, out[RHS:], out[:RHS])

    def store_split(ref, at, matrix):
        high, low = halves(matrix)
        ref[at, : 2 * RANK] = high
        ref[at, 2 * RANK :] = low

    loads["top_transfer"].wait()
    loads["top_coupling"].wait()
    for step in range(levels_top):
        block = top_coupling[step]
        store_split(top_field_w, step, jnp.concatenate([block, block], axis=0).T)
        if step + 1 < levels_top:
            block = top_transfer[step]
            twice = jnp.concatenate([block, block], axis=0)
            store_split(top_up_w, step, twice.T)
            store_split(top_down_w, step, twice)

    rim_copies = [[] for _ in range(LOC_LEVELS)]

    def send_rim(h):
        count = RIM_PAIRS[h]
        at = RIM_AT[h]
        first = PAIR_AT[h]
        last = first + COUNTS[h] // 2 - count
        for side, (other, start) in enumerate(((right, last), (left, first))):
            copy = pltpu.make_async_remote_copy(
                src_ref=pairs.at[pl.ds(start, count)],
                dst_ref=rim.at[side, pl.ds(at, count)],
                send_sem=rim_ssem.at[side, h],
                recv_sem=rim_rsem.at[side, h],
                device_id=(other,),
                device_id_type=MESH,
            )
            copy.start()
            rim_copies[h].append(copy)

    def widen(h, slot, pair, which):
        turned = pltpu.roll(pair, RANK, 1)
        if which != 1:
            wide[WIDE_AT[h] + slot] = jnp.where(lane_high, turned, pair)
        if which != 0:
            wide[WIDE_AT[h] + slot + (which == 2)] = jnp.where(lane_high, pair, turned)

    loads["values"].wait()
    loads["basis"].wait()

    def leaf_pair(j, _):
        at = pl.multiple_of(j * 2 * LEAF_PTS, 2 * LEAF_PTS)
        x = values[:, pl.ds(at, 2 * LEAF_PTS)]
        v = basis[:, pl.ds(at, 2 * LEAF_PTS)]
        out = times_t(
            jnp.concatenate([x[:, :LEAF_PTS], x[:, LEAF_PTS:]], axis=0),
            jnp.concatenate([v[:, :LEAF_PTS], v[:, LEAF_PTS:]], axis=0),
        )
        pair = join(out)
        pairs[j] = pair
        widen(0, RIMS[0] + 2 * j, pair, 2)
        return 0

    lax.fori_loop(0, LEAVES_DEV // 2, leaf_pair, 0, unroll=UNROLL)
    loads["points"].wait()
    for side in range(2):
        for e in range(FACE):
            leaf = face_leaf(1 - side, e)
            at = leaf * LEAF_PTS
            face_x[side, e] = values[:, at : at + LEAF_PTS]
            for axis in range(3):
                face_p[side, axis, e : e + 1, :] = points[axis : axis + 1, at : at + LEAF_PTS]
    pl.semaphore_wait(barrier, greeted)
    face_copies = []
    for side, other in ((0, right), (1, left)):
        for n, (src, dst) in enumerate(((face_x, halo_x), (face_p, halo_p))):
            copy = pltpu.make_async_remote_copy(
                src_ref=src.at[side],
                dst_ref=dst.at[side],
                send_sem=face_send.at[side, n],
                recv_sem=face_recv.at[side, n],
                device_id=(other,),
                device_id_type=MESH,
            )
            copy.start()
            face_copies.append(copy)

    send_rim(0)
    loads["transfer"].wait()
    for h in range(1, LOC_LEVELS):

        def node_pair(j, _, h=h):
            below = pairs[pl.ds(PAIR_AT[h - 1] + 2 * j, 2)].reshape(2 * RHS, 2 * RANK)
            weights = transfer[pl.ds(TRANSFER_AT[h] + 2 * j, 2)].reshape(2 * RANK, 2 * RANK)
            pair = join(times_t(below, weights))
            pairs[PAIR_AT[h] + j] = pair
            widen(h, RIMS[h] + 2 * j, pair, 2)
            return 0

        total = COUNTS[h] // 2
        lax.fori_loop(0, total, node_pair, 0, unroll=min(UNROLL, total))
        send_rim(h)
    root = transfer[LEAVES_DEV - 2]
    root_twice = jnp.concatenate([root, root], axis=0)
    current = times_t(pairs[PAIR_AT[LOC_LEVELS - 1]], root_twice)

    def couple_level(h):
        for copy in rim_copies[h]:
            copy.wait()
        if RIMS[h] == 1:
            widen(h, 0, rim[0, RIM_AT[h]], 1)
            widen(h, 1 + COUNTS[h], rim[1, RIM_AT[h]], 0)
        else:
            for n in range(RIM_PAIRS[h]):
                widen(h, 2 * n, rim[0, RIM_AT[h] + n], 2)
                widen(h, RIMS[h] + COUNTS[h] + 2 * n, rim[1, RIM_AT[h] + n], 2)

        def couple(j, _, h=h):
            start = RIMS[h] - me * COUNTS[h]
            last = COUNTS[h] + 2 * RIMS[h] - 1
            rows = []
            for n in range(2):
                k = COUPLING_AT[h] + 2 * j + n
                first = wide[WIDE_AT[h] + jnp.clip(partners[0, k] + start, 0, last)]
                second = wide[WIDE_AT[h] + jnp.clip(partners[1, k] + start, 0, last)]
                rows.append(jnp.where(lane_high, second, first))
            weights = coupling[pl.ds(COUPLING_AT[h] + 2 * j, 2)].reshape(2 * RANK, 2 * RANK)
            field[PAIR_AT[h] + j] = join(times_t(jnp.concatenate(rows, axis=0), weights))
            return 0

        total = COUNTS[h] // 2
        lax.fori_loop(0, total, couple, 0, unroll=min(UNROLL, total))

    def three(a):
        high = a.astype(bf16).astype(f32)
        rest = a - high
        mid = rest.astype(bf16).astype(f32)
        return high, mid, rest - mid

    def lay_parts(at, width, coords):
        lanes = pl.ds(at, width)
        square = coords * coords
        norm = three(square[0:1] + square[1:2] + square[2:3])
        for n, part in enumerate(three(coords)):
            parts[3 * n : 3 * n + 3, lanes] = part
            parts[9 + n : 10 + n, lanes] = norm[n]

    def chosen(shape, row_dim, pairs_of):
        row = lax.broadcasted_iota(jnp.int32, shape, row_dim)
        term = lax.broadcasted_iota(jnp.int32, shape, 1 - row_dim)
        out = jnp.zeros(shape, f32)
        for k, (r, factor) in pairs_of.items():
            out = jnp.where((term == k) & (row == r), factor, out)
        return out.astype(bf16)

    of_target, of_source = {}, {}
    for axis in range(3):
        for n, (s, t) in enumerate(((0, 0), (0, 1), (1, 0), (0, 2), (2, 0), (1, 1))):
            of_source[3 * n + axis] = (3 * s + axis, 1.0)
            of_target[3 * n + axis] = (3 * t + axis, -2.0)
        of_source[18 + axis] = (9 + axis, 1.0)
        of_target[18 + axis] = (12, 1.0)
        of_source[21 + axis] = (12, 1.0)
        of_target[21 + axis] = (9 + axis, 1.0)

    axis_id = lax.broadcasted_iota(jnp.int32, (3, 1), 0)
    centre = jnp.where(axis_id == 0, (me * 4 + 2).astype(f32), 2.0)

    def lay_source(n):
        at = pl.multiple_of(n * LEAF_PTS, LEAF_PTS)
        turned = parts[:, pl.ds(at, LEAF_PTS)].T.astype(bf16)
        pick_low = chosen((16, 2 * TERMS), 0, of_source)
        pick_high = chosen((16, 2 * TERMS), 0, {k + TERMS: v for k, v in of_source.items()})
        source_low[n] = jnp.dot(turned, pick_low, preferred_element_type=f32).astype(bf16)
        source_high[n] = jnp.dot(turned, pick_high, preferred_element_type=f32).astype(bf16)

    def lay_rhs(n, x):
        high, low = halves(x)
        rhs[n, :RHS] = high
        rhs[n, RHS:] = low

    def prepare_own():
        parts[12:16, :] = jnp.where(
            lax.broadcasted_iota(jnp.int32, (4, SOURCES * LEAF_PTS), 0) == 0, 1.0, 0.0
        )
        lay_parts(0, LEAVES_DEV * LEAF_PTS, (points[...] - centre) * SCALE)
        rhs[SOURCES] = jnp.zeros((2 * RHS, LEAF_PTS), bf16)
        squares[...] = jnp.zeros_like(squares)
        entries_high[...] = jnp.zeros_like(entries_high)
        entries_low[...] = jnp.zeros_like(entries_low)

        def one(n, _):
            lanes = pl.ds(pl.multiple_of(n * LEAF_PTS, LEAF_PTS), LEAF_PTS)
            pick = chosen((TERMS, 16), 1, of_target)
            terms = jnp.dot(pick, parts[:, lanes].astype(bf16), preferred_element_type=f32)
            terms = terms.astype(bf16)
            none = jnp.zeros_like(terms)
            target[n, :TERMS, :LEAF_PTS] = terms
            target[n, :TERMS, LEAF_PTS:] = none
            target[n, TERMS:, :LEAF_PTS] = none
            target[n, TERMS:, LEAF_PTS:] = terms
            lay_source(n)
            lay_rhs(n, values[:, lanes])
            return 0

        lax.fori_loop(0, LEAVES_DEV, one, 0, unroll=UNROLL)

    def prepare_faces():
        for copy in face_copies:
            copy.wait()
        for side in range(2):
            for e in range(FACE):
                at = (LEAVES_DEV + side * FACE + e) * LEAF_PTS
                coords = jnp.concatenate(
                    [halo_p[side, axis, e : e + 1, :] for axis in range(3)], axis=0
                )
                lay_parts(at, LEAF_PTS, (coords - centre) * SCALE)

        def one(e, _):
            for side in range(2):
                lay_source(LEAVES_DEV + side * FACE + e)
                lay_rhs(LEAVES_DEV + side * FACE + e, halo_x[side, e])
            return 0

        lax.fori_loop(0, FACE, one, 0, unroll=UNROLL // 2)

    def leaf_at(i):
        side = (i >> 4) & 1
        inside = jnp.where(side == 0, 1, 8)
        return face_leaf(0, i & 15) + jnp.where(i < LEAVES_DEV // 2, inside, 9 * side)

    def slot_source(leaf, slot):
        column = columns[slot, leaf] - me * LEAVES_DEV
        inner = column & (LEAVES_DEV - 1)
        face = ((inner >> 1) & 3) | (((inner >> 4) & 3) << 2)
        beyond = jnp.where(column < 0, LEAVES_DEV + face, LEAVES_DEV + FACE + face)
        return jnp.where((column >= 0) & (column < LEAVES_DEV), column, beyond)

    def near_step(i, now, later):
        done = leaf_at(jnp.maximum(i - 2, 0))
        live = counts[done]
        total = None
        for p in range(NEAR_SLOTS // 2):
            x = jnp.concatenate(
                [
                    rhs[jnp.where(slot < live, slot_source(done, slot), SOURCES)]
                    for slot in (2 * p, 2 * p + 1)
                ],
                axis=1,
            )
            rows = slice(2 * p * LEAF_PTS, 2 * (p + 1) * LEAF_PTS)
            both = jnp.dot(x, entries_high[now, rows], preferred_element_type=f32)
            rest = jnp.dot(x[:RHS], entries_low[now, rows], preferred_element_type=f32)
            out = both[:RHS] + (both[RHS:] + rest)
            total = out if total is None else total + out
        for p in range(NEAR_SLOTS // 2):
            for n in range(2):
                square = squares[now, p, :, n * LEAF_PTS : (n + 1) * LEAF_PTS]
                square = jnp.maximum(square, 1e-12)
                t = square * lax.rsqrt(square)
                high, low = halves((t + LOG2E) * jnp.exp2(-t))
                rows = slice((2 * p + n) * LEAF_PTS, (2 * p + n + 1) * LEAF_PTS)
                entries_high[later, rows] = high
                entries_low[later, rows] = low
        leaf = leaf_at(jnp.minimum(i, LEAVES_DEV - 1))
        left = jnp.concatenate(
            [
                source_low[slot_source(leaf, 2 * p)] + source_high[slot_source(leaf, 2 * p + 1)]
                for p in range(NEAR_SLOTS // 2)
            ],
            axis=0,
        )
        out = jnp.dot(left, target[leaf], preferred_element_type=f32)
        for p in range(NEAR_SLOTS // 2):
            squares[later, p] = out[p * LEAF_PTS : (p + 1) * LEAF_PTS]
        at = pl.multiple_of(done * LEAF_PTS, LEAF_PTS)
        far[:, pl.ds(at, LEAF_PTS)] = AMPLITUDE * total

    def near_steps(first, last):
        def two(j, _):
            near_step(2 * j, 0, 1)
            near_step(2 * j + 1, 1, 0)
            return 0

        lax.fori_loop(first // 2, last // 2, two, 0)

    half = (lax.broadcasted_iota(jnp.int32, (RHS, 2 * RANK), 1) >= RANK).astype(jnp.int32)
    top_field = []
    for r, (base, bits) in enumerate(rounds):
        packed[r] = jnp.where(lane_high[: RHS // 2], current[RHS // 2 :], current[: RHS // 2])
        copies = []
        for k in range(1, 1 << bits):
            copy = pltpu.make_async_remote_copy(
                src_ref=packed.at[r],
                dst_ref=gathered.at[r, k],
                send_sem=top_send.at[r, k],
                recv_sem=top_recv.at[r, k],
                device_id=(me ^ (k << base),),
                device_id_type=MESH,
            )
            copy.start()
            copies.append(copy)
        if r == 0:
            prepare_own()
            loads["coupling"].wait()
            couple_level(0)
            near_steps(0, LEAVES_DEV // 2)
        if r == len(rounds) - 1:
            prepare_faces()
            for h in range(1, LOC_LEVELS):
                couple_level(h)
            near_steps(LEAVES_DEV // 2, LEAVES_DEV + 2)
        for copy in copies:
            copy.wait()
        nodes = [current]
        for k in range(1, 1 << bits):
            got = gathered[r, k]
            turned = pltpu.roll(got, RANK, 1)
            low = lane_high[: RHS // 2]
            nodes.append(
                jnp.concatenate(
                    [jnp.where(low, turned, got), jnp.where(low, got, turned)], axis=0
                )
            )
        for step in range(base, base + bits):
            own_half = half == ((me >> step) & 1)
            top_field.append(apply(jnp.where(own_half, nodes[1], 0.0), top_field_w[step]))
            if step + 1 < levels_top:
                is_left = half == ((me >> step) & 1)
                joined = [
                    jnp.where(is_left, nodes[2 * j], nodes[2 * j + 1])
                    for j in range(len(nodes) // 2)
                ]
                out = apply(jnp.concatenate(joined, axis=0), top_up_w[step])
                nodes = [out[RHS * j : RHS * (j + 1)] for j in range(len(joined))]
                current = nodes[0]

    spread = jnp.where(half == 0, top_field[-1], 0.0)
    for step in reversed(range(levels_top - 1)):
        out = apply(spread, top_down_w[step])
        spread = jnp.where(half == ((me >> step) & 1), out + top_field[step], 0.0)
    out = times(spread, root_twice)
    down[PAIR_AT[LOC_LEVELS - 1]] = out + field[PAIR_AT[LOC_LEVELS - 1]]

    def apart(pair):
        return jnp.concatenate(
            [jnp.where(lane_high, 0.0, pair), jnp.where(lane_high, pair, 0.0)], axis=0
        )

    for h in range(LOC_LEVELS - 1, 0, -1):

        def descend(j, _, h=h):
            weights = transfer[pl.ds(TRANSFER_AT[h] + 2 * j, 2)].reshape(2 * RANK, 2 * RANK)
            out = times(apart(down[PAIR_AT[h] + j]), weights)
            below = PAIR_AT[h - 1] + 2 * j
            down[below] = out[:RHS] + field[below]
            down[below + 1] = out[RHS:] + field[below + 1]
            return 0

        total = COUNTS[h] // 2
        lax.fori_loop(0, total, descend, 0, unroll=min(UNROLL, total))

    def expand(j, _):
        at = pl.multiple_of(j * 2 * LEAF_PTS, 2 * LEAF_PTS)
        v = basis[:, pl.ds(at, 2 * LEAF_PTS)]
        out = times(
            apart(down[j]), jnp.concatenate([v[:, :LEAF_PTS], v[:, LEAF_PTS:]], axis=0)
        )
        far[:, pl.ds(at, LEAF_PTS)] += out[:RHS]
        far[:, pl.ds(at + LEAF_PTS, LEAF_PTS)] += out[RHS:]
        return 0

    lax.fori_loop(0, LEAVES_DEV // 2, expand, 0, unroll=UNROLL)


def product_of(
    devices,
    values,
    points,
    basis,
    transfer,
    coupling,
    top_transfer,
    top_coupling,
    partners,
    columns,
    counts,
):
    leaf_points = LEAVES_DEV * LEAF_PTS
    rounds = rounds_of(devices)
    width = 1 << ROUND_BITS
    return pl.pallas_call(
        functools.partial(kernel, devices),
        out_shape=jax.ShapeDtypeStruct((RHS, leaf_points), f32),
        in_specs=[pl.BlockSpec(memory_space=pl.ANY)] * 7
        + [pl.BlockSpec(memory_space=pltpu.SMEM)] * 3,
        out_specs=pl.BlockSpec(memory_space=pltpu.VMEM),
        scratch_shapes=[
            pltpu.VMEM((2, FACE, RHS, LEAF_PTS), f32),
            pltpu.VMEM((2, 3, FACE, LEAF_PTS), f32),
            pltpu.VMEM((RHS, leaf_points), f32),
            pltpu.VMEM((3, leaf_points), f32),
            pltpu.VMEM((RANK, leaf_points), f32),
            pltpu.VMEM(transfer.shape, f32),
            pltpu.VMEM(coupling.shape, f32),
            pltpu.VMEM(top_transfer.shape, f32),
            pltpu.VMEM(top_coupling.shape, f32),
            pltpu.VMEM((2, FACE, RHS, LEAF_PTS), f32),
            pltpu.VMEM((2, 3, FACE, LEAF_PTS), f32),
            pltpu.VMEM((LEAVES_DEV - 1, RHS, 2 * RANK), f32),
            pltpu.VMEM((2, sum(RIM_PAIRS), RHS, 2 * RANK), f32),
            pltpu.VMEM((WIDE_AT[-1], RHS, 2 * RANK), f32),
            pltpu.VMEM((LEAVES_DEV - 1, RHS, 2 * RANK), f32),
            pltpu.VMEM((LEAVES_DEV - 1, RHS, 2 * RANK), f32),
            pltpu.VMEM((len(rounds), RHS // 2, 2 * RANK), f32),
            pltpu.VMEM((len(rounds), width, RHS // 2, 2 * RANK), f32),
            pltpu.VMEM((top_transfer.shape[0], 4 * RANK, 2 * RANK), bf16),
            pltpu.VMEM((top_transfer.shape[0], 4 * RANK, 2 * RANK), bf16),
            pltpu.VMEM((top_coupling.shape[0], 4 * RANK, 2 * RANK), bf16),
            pltpu.VMEM((16, SOURCES * LEAF_PTS), f32),
            pltpu.VMEM((LEAVES_DEV, 2 * TERMS, 2 * LEAF_PTS), bf16),
            pltpu.VMEM((SOURCES, LEAF_PTS, 2 * TERMS), bf16),
            pltpu.VMEM((SOURCES, LEAF_PTS, 2 * TERMS), bf16),
            pltpu.VMEM((SOURCES + 1, 2 * RHS, LEAF_PTS), bf16),
            pltpu.VMEM((2, NEAR_SLOTS // 2, LEAF_PTS, 2 * LEAF_PTS), f32),
            pltpu.VMEM((2, NEAR_SLOTS * LEAF_PTS, LEAF_PTS), bf16),
            pltpu.VMEM((2, NEAR_SLOTS * LEAF_PTS, LEAF_PTS), bf16),
            pltpu.SemaphoreType.DMA((7,)),
            pltpu.SemaphoreType.DMA((2, 2)),
            pltpu.SemaphoreType.DMA((2, 2)),
            pltpu.SemaphoreType.DMA((2, LOC_LEVELS)),
            pltpu.SemaphoreType.DMA((2, LOC_LEVELS)),
            pltpu.SemaphoreType.DMA((len(rounds), width)),
            pltpu.SemaphoreType.DMA((len(rounds), width)),
        ],
        compiler_params=pltpu.CompilerParams(
            collective_id=0, has_side_effects=True, vmem_limit_bytes=60 << 20
        ),
        name="h2_product",
    )(
        values,
        points,
        basis,
        transfer,
        coupling,
        top_transfer,
        top_coupling,
        partners,
        columns,
        counts,
    )


def local(
    values,
    points,
    basis,
    local_transfer,
    local_coupling,
    local_partners,
    top_transfer,
    top_coupling,
    near_cols,
    near_count,
):
    devices = lax.axis_size("leaf")
    return product_of(
        devices,
        values,
        points,
        basis,
        local_transfer,
        local_coupling,
        top_transfer,
        top_coupling,
        local_partners.T,
        near_cols.T,
        near_count,
    )


def solution(mesh):
    placed = (
        P(None, "leaf"),
        P(None, "leaf"),
        P(None, "leaf"),
        P("leaf", None, None),
        P("leaf", None, None),
        P("leaf", None),
        P(),
        P(),
        P("leaf", None),
        P("leaf"),
    )
    return jax.shard_map(
        local, mesh=mesh, in_specs=placed, out_specs=P(None, "leaf"), check_vma=False
    )
```

```python
import functools
import math

import jax
import jax.numpy as jnp
import numpy as np
from jax import lax
from jax.experimental import pallas as pl
from jax.experimental.pallas import tpu as pltpu
from jax.sharding import PartitionSpec as P

LEAF_PTS = 128
RANK = 64
RHS = 32
NEAR_SLOTS = 8
COUPLE = 2
WINDOW = 4
LOC_LEVELS = 6
LEAVES_DEV = 64
FACE = 16
SOURCES = LEAVES_DEV + 2 * FACE
ROUND_BITS = 4
TERMS = 32
UNROLL = 8
NEAR_FIRST = 0

MESH = pl.DeviceIdType.MESH
bf16 = jnp.bfloat16
f32 = jnp.float32
LOG2E = 1.4426950408889634
SCALE = math.sqrt(3.0) / 0.5 * LOG2E
AMPLITUDE = 0.25 / LOG2E

COUNTS = [LEAVES_DEV >> h for h in range(LOC_LEVELS + 1)]
RIMS = [min(WINDOW, (LEAVES_DEV >> h) // 2) for h in range(LOC_LEVELS)]
PAIR_AT = [LEAVES_DEV - COUNTS[h] for h in range(LOC_LEVELS)]
RIM_PAIRS = [max(1, r // 2) for r in RIMS]
RIM_AT = [sum(RIM_PAIRS[:h]) for h in range(LOC_LEVELS)]
WIDE_AT = [sum(COUNTS[g] + 2 * RIMS[g] for g in range(h)) for h in range(LOC_LEVELS + 1)]
TRANSFER_AT = [LEAVES_DEV - 2 * c for c in COUNTS]
COUPLING_AT = [2 * LEAVES_DEV - 2 * c for c in COUNTS]


def rounds_of(devices):
    total = devices.bit_length() - 1
    return [(b, min(ROUND_BITS, total - b)) for b in range(0, total, ROUND_BITS)]


def halves(a):
    high = a.astype(bf16)
    return high, (a - high.astype(f32)).astype(bf16)


def doubled(left):
    high, low = halves(left)
    return jnp.concatenate(
        [
            jnp.concatenate([high, high], axis=1),
            jnp.concatenate([low, jnp.zeros_like(low)], axis=1),
        ],
        axis=0,
    )


def apply(left, stacked):
    rows = left.shape[0]
    out = jnp.dot(doubled(left), stacked, preferred_element_type=f32)
    return out[:rows] + out[rows:]


def times(left, right):
    return apply(left, jnp.concatenate(halves(right), axis=0))


def times_t(left, right):
    rows = left.shape[0]
    out = lax.dot_general(
        doubled(left),
        jnp.concatenate(halves(right), axis=1),
        (((1,), (1,)), ((), ())),
        preferred_element_type=f32,
    )
    return out[:rows] + out[rows:]


def face_leaf(side, e):
    spread = ((e & 3) << 1) | ((e >> 2) << 4)
    return spread + 9 * side


def kernel(
    devices,
    values_h,
    points_h,
    basis_h,
    transfer_h,
    coupling_h,
    top_transfer_h,
    top_coupling_h,
    partners,
    columns,
    counts,
    far,
    halo_x,
    halo_p,
    values,
    points,
    basis,
    transfer,
    coupling,
    top_transfer,
    top_coupling,
    face_x,
    face_p,
    pairs,
    rim,
    wide,
    field,
    down,
    packed,
    gathered,
    top_up_w,
    top_down_w,
    top_field_w,
    parts,
    target,
    source,
    rhs,
    squares,
    entries_high,
    entries_low,
    load_sem,
    face_send,
    face_recv,
    rim_ssem,
    rim_rsem,
    top_send,
    top_recv,
):
    me = lax.axis_index("leaf")
    right = lax.rem(me + 1, devices)
    left = lax.rem(me + devices - 1, devices)
    rounds = rounds_of(devices)
    levels_top = devices.bit_length() - 1

    barrier = pltpu.get_barrier_semaphore()
    greeted = 0
    for other in (left, right):
        pl.semaphore_signal(barrier, inc=1, device_id=(other,), device_id_type=MESH)
        greeted += 1
    for base, bits in rounds:
        for k in range(1, 1 << bits):
            pl.semaphore_signal(
                barrier, inc=1, device_id=(me ^ (k << base),), device_id_type=MESH
            )
            greeted += 1

    loads = {}
    for n, (name, src, dst) in enumerate(
        [
            ("top_transfer", top_transfer_h, top_transfer),
            ("top_coupling", top_coupling_h, top_coupling),
            ("values", values_h, values),
            ("basis", basis_h, basis),
            ("points", points_h, points),
            ("transfer", transfer_h, transfer),
            ("coupling", coupling_h, coupling),
        ]
    ):
        loads[name] = pltpu.make_async_copy(src, dst, load_sem.at[n])
        loads[name].start()

    lane_high = lax.broadcasted_iota(jnp.int32, (RHS, 2 * RANK), 1) >= RANK

    def join(out):
        return jnp.where(lane_high, out[RHS:], out[:RHS])

    def store_split(ref, at, matrix):
        high, low = halves(matrix)
        ref[at, : 2 * RANK] = high
        ref[at, 2 * RANK :] = low

    loads["top_transfer"].wait()
    loads["top_coupling"].wait()
    for step in range(levels_top):
        block = top_coupling[step]
        store_split(top_field_w, step, jnp.concatenate([block, block], axis=0).T)
        if step + 1 < levels_top:
            block = top_transfer[step]
            twice = jnp.concatenate([block, block], axis=0)
            store_split(top_up_w, step, twice.T)
            store_split(top_down_w, step, twice)

    rim_copies = [[] for _ in range(LOC_LEVELS)]

    def send_rim(h):
        count = RIM_PAIRS[h]
        at = RIM_AT[h]
        first = PAIR_AT[h]
        last = first + COUNTS[h] // 2 - count
        for side, (other, start) in enumerate(((right, last), (left, first))):
            copy = pltpu.make_async_remote_copy(
                src_ref=pairs.at[pl.ds(start, count)],
                dst_ref=rim.at[side, pl.ds(at, count)],
                send_sem=rim_ssem.at[side, h],
                recv_sem=rim_rsem.at[side, h],
                device_id=(other,),
                device_id_type=MESH,
            )
            copy.start()
            rim_copies[h].append(copy)

    def widen(h, slot, pair, which):
        turned = pltpu.roll(pair, RANK, 1)
        if which != 1:
            wide[WIDE_AT[h] + slot] = jnp.where(lane_high, turned, pair)
        if which != 0:
            wide[WIDE_AT[h] + slot + (which == 2)] = jnp.where(lane_high, pair, turned)

    loads["values"].wait()
    loads["basis"].wait()

    def leaf_pair(j, _):
        at = pl.multiple_of(j * 2 * LEAF_PTS, 2 * LEAF_PTS)
        x = values[:, pl.ds(at, 2 * LEAF_PTS)]
        v = basis[:, pl.ds(at, 2 * LEAF_PTS)]
        out = times_t(
            jnp.concatenate([x[:, :LEAF_PTS], x[:, LEAF_PTS:]], axis=0),
            jnp.concatenate([v[:, :LEAF_PTS], v[:, LEAF_PTS:]], axis=0),
        )
        pair = join(out)
        pairs[j] = pair
        widen(0, RIMS[0] + 2 * j, pair, 2)
        return 0

    lax.fori_loop(0, LEAVES_DEV // 2, leaf_pair, 0, unroll=UNROLL)
    loads["points"].wait()
    for side in range(2):
        for e in range(FACE):
            leaf = face_leaf(1 - side, e)
            at = leaf * LEAF_PTS
            face_x[side, e] = values[:, at : at + LEAF_PTS]
            for axis in range(3):
                face_p[side, axis, e : e + 1, :] = points[axis : axis + 1, at : at + LEAF_PTS]
    loads["transfer"].wait()
    for h in range(1, LOC_LEVELS):

        def node_pair(j, _, h=h):
            below = pairs[pl.ds(PAIR_AT[h - 1] + 2 * j, 2)].reshape(2 * RHS, 2 * RANK)
            weights = transfer[pl.ds(TRANSFER_AT[h] + 2 * j, 2)].reshape(2 * RANK, 2 * RANK)
            pair = join(times_t(below, weights))
            pairs[PAIR_AT[h] + j] = pair
            widen(h, RIMS[h] + 2 * j, pair, 2)
            return 0

        total = COUNTS[h] // 2
        lax.fori_loop(0, total, node_pair, 0, unroll=min(UNROLL, total))
    root = transfer[LEAVES_DEV - 2]
    root_twice = jnp.concatenate([root, root], axis=0)
    current = times_t(pairs[PAIR_AT[LOC_LEVELS - 1]], root_twice)

    def couple_level(h):
        for copy in rim_copies[h]:
            copy.wait()
        if RIMS[h] == 1:
            widen(h, 0, rim[0, RIM_AT[h]], 1)
            widen(h, 1 + COUNTS[h], rim[1, RIM_AT[h]], 0)
        else:
            for n in range(RIM_PAIRS[h]):
                widen(h, 2 * n, rim[0, RIM_AT[h] + n], 2)
                widen(h, RIMS[h] + COUNTS[h] + 2 * n, rim[1, RIM_AT[h] + n], 2)

        def couple(j, _, h=h):
            start = RIMS[h] - me * COUNTS[h]
            last = COUNTS[h] + 2 * RIMS[h] - 1
            rows = []
            for n in range(2):
                k = COUPLING_AT[h] + 2 * j + n
                first = wide[WIDE_AT[h] + jnp.clip(partners[0, k] + start, 0, last)]
                second = wide[WIDE_AT[h] + jnp.clip(partners[1, k] + start, 0, last)]
                rows.append(jnp.where(lane_high, second, first))
            weights = coupling[pl.ds(COUPLING_AT[h] + 2 * j, 2)].reshape(2 * RANK, 2 * RANK)
            field[PAIR_AT[h] + j] = join(times_t(jnp.concatenate(rows, axis=0), weights))
            return 0

        total = COUNTS[h] // 2
        lax.fori_loop(0, total, couple, 0, unroll=min(UNROLL, total))

    def three(a):
        high = a.astype(bf16).astype(f32)
        rest = a - high
        mid = rest.astype(bf16).astype(f32)
        return high, mid, rest - mid

    def lay_parts(at, width, coords):
        lanes = pl.ds(at, width)
        square = coords * coords
        norm = three(square[0:1] + square[1:2] + square[2:3])
        for n, part in enumerate(three(coords)):
            parts[3 * n : 3 * n + 3, lanes] = part
            parts[9 + n : 10 + n, lanes] = norm[n]

    def chosen(shape, row_dim, pairs_of):
        row = lax.broadcasted_iota(jnp.int32, shape, row_dim)
        term = lax.broadcasted_iota(jnp.int32, shape, 1 - row_dim)
        out = jnp.zeros(shape, f32)
        for k, (r, factor) in pairs_of.items():
            out = jnp.where((term == k) & (row == r), factor, out)
        return out.astype(bf16)

    of_target, of_source = {}, {}
    for axis in range(3):
        for n, (s, t) in enumerate(((0, 0), (0, 1), (1, 0), (0, 2), (2, 0), (1, 1))):
            of_source[3 * n + axis] = (3 * s + axis, 1.0)
            of_target[3 * n + axis] = (3 * t + axis, -2.0)
        of_source[18 + axis] = (9 + axis, 1.0)
        of_target[18 + axis] = (12, 1.0)
        of_source[21 + axis] = (12, 1.0)
        of_target[21 + axis] = (9 + axis, 1.0)

    axis_id = lax.broadcasted_iota(jnp.int32, (3, 1), 0)
    centre = jnp.where(axis_id == 0, (me * 4 + 2).astype(f32), 2.0)

    def lay_source(n):
        at = pl.multiple_of(n * LEAF_PTS, LEAF_PTS)
        turned = parts[:, pl.ds(at, LEAF_PTS)].T.astype(bf16)
        pick = chosen((16, TERMS), 0, of_source)
        source[n] = jnp.dot(turned, pick, preferred_element_type=f32).astype(bf16)

    def lay_rhs(n, x):
        high, low = halves(x)
        rhs[n, :RHS] = high
        rhs[n, RHS:] = low

    def prepare_own():
        parts[12:16, :] = jnp.where(
            lax.broadcasted_iota(jnp.int32, (4, SOURCES * LEAF_PTS), 0) == 0, 1.0, 0.0
        )
        lay_parts(0, LEAVES_DEV * LEAF_PTS, (points[...] - centre) * SCALE)
        rhs[SOURCES] = jnp.zeros((2 * RHS, LEAF_PTS), bf16)
        squares[...] = jnp.zeros_like(squares)
        entries_high[...] = jnp.zeros_like(entries_high)
        entries_low[...] = jnp.zeros_like(entries_low)

        def one(n, _):
            lanes = pl.ds(pl.multiple_of(n * LEAF_PTS, LEAF_PTS), LEAF_PTS)
            pick = chosen((TERMS, 16), 1, of_target)
            terms = jnp.dot(pick, parts[:, lanes].astype(bf16), preferred_element_type=f32)
            target[n] = terms.astype(bf16)
            lay_source(n)
            lay_rhs(n, values[:, lanes])
            return 0

        lax.fori_loop(0, LEAVES_DEV, one, 0, unroll=UNROLL)

    def prepare_faces():
        for copy in face_copies:
            copy.wait()
        for side in range(2):
            for e in range(FACE):
                at = (LEAVES_DEV + side * FACE + e) * LEAF_PTS
                coords = jnp.concatenate(
                    [halo_p[side, axis, e : e + 1, :] for axis in range(3)], axis=0
                )
                lay_parts(at, LEAF_PTS, (coords - centre) * SCALE)

        def one(e, _):
            for side in range(2):
                lay_source(LEAVES_DEV + side * FACE + e)
                lay_rhs(LEAVES_DEV + side * FACE + e, halo_x[side, e])
            return 0

        lax.fori_loop(0, FACE, one, 0, unroll=UNROLL // 2)

    def leaf_at(i):
        side = (i >> 4) & 1
        inside = jnp.where(side == 0, 1, 8)
        return face_leaf(0, i & 15) + jnp.where(i < LEAVES_DEV // 2, inside, 9 * side)

    def slot_source(leaf, slot):
        column = columns[slot, leaf] - me * LEAVES_DEV
        inner = column & (LEAVES_DEV - 1)
        face = ((inner >> 1) & 3) | (((inner >> 4) & 3) << 2)
        beyond = jnp.where(column < 0, LEAVES_DEV + face, LEAVES_DEV + FACE + face)
        return jnp.where((column >= 0) & (column < LEAVES_DEV), column, beyond)

    def near_step(i, now, later):
        done = leaf_at(jnp.maximum(i - 2, 0))
        live = counts[done]
        total = None
        for p in range(NEAR_SLOTS // 2):
            x = jnp.concatenate(
                [
                    rhs[jnp.where(slot < live, slot_source(done, slot), SOURCES)]
                    for slot in (2 * p, 2 * p + 1)
                ],
                axis=1,
            )
            rows = slice(2 * p * LEAF_PTS, 2 * (p + 1) * LEAF_PTS)
            both = jnp.dot(x, entries_high[now, rows], preferred_element_type=f32)
            rest = jnp.dot(x[:RHS], entries_low[now, rows], preferred_element_type=f32)
            out = both[:RHS] + (both[RHS:] + rest)
            total = out if total is None else total + out
        for p in range(NEAR_SLOTS // 2):
            square = jnp.maximum(squares[now, p], 1e-12)
            t = square * lax.rsqrt(square)
            high, low = halves((t + LOG2E) * jnp.exp2(-t))
            rows = slice(2 * p * LEAF_PTS, 2 * (p + 1) * LEAF_PTS)
            entries_high[later, rows] = high
            entries_low[later, rows] = low
        leaf = leaf_at(jnp.minimum(i, LEAVES_DEV - 1))
        left = jnp.concatenate(
            [source[slot_source(leaf, slot)] for slot in range(NEAR_SLOTS)], axis=0
        )
        out = jnp.dot(left, target[leaf], preferred_element_type=f32)
        for p in range(NEAR_SLOTS // 2):
            squares[later, p] = out[2 * p * LEAF_PTS : 2 * (p + 1) * LEAF_PTS]
        at = pl.multiple_of(done * LEAF_PTS, LEAF_PTS)
        far[:, pl.ds(at, LEAF_PTS)] = AMPLITUDE * total

    def near_steps(first, last):
        def two(j, _):
            near_step(2 * j, 0, 1)
            near_step(2 * j + 1, 1, 0)
            return 0

        lax.fori_loop(first // 2, last // 2, two, 0)

    half = (lax.broadcasted_iota(jnp.int32, (RHS, 2 * RANK), 1) >= RANK).astype(jnp.int32)
    top_field = []
    prepare_own()
    near_steps(0, NEAR_FIRST)
    pl.semaphore_wait(barrier, greeted)
    face_copies = []
    for side, other in ((0, right), (1, left)):
        for n, (src, dst) in enumerate(((face_x, halo_x), (face_p, halo_p))):
            copy = pltpu.make_async_remote_copy(
                src_ref=src.at[side],
                dst_ref=dst.at[side],
                send_sem=face_send.at[side, n],
                recv_sem=face_recv.at[side, n],
                device_id=(other,),
                device_id_type=MESH,
            )
            copy.start()
            face_copies.append(copy)

    for h in range(LOC_LEVELS):
        send_rim(h)
    for r, (base, bits) in enumerate(rounds):
        packed[r] = jnp.where(lane_high[: RHS // 2], current[RHS // 2 :], current[: RHS // 2])
        copies = []
        for k in range(1, 1 << bits):
            copy = pltpu.make_async_remote_copy(
                src_ref=packed.at[r],
                dst_ref=gathered.at[r, k],
                send_sem=top_send.at[r, k],
                recv_sem=top_recv.at[r, k],
                device_id=(me ^ (k << base),),
                device_id_type=MESH,
            )
            copy.start()
            copies.append(copy)
        if r == 0:
            near_steps(NEAR_FIRST, LEAVES_DEV // 2)
            loads["coupling"].wait()
            couple_level(0)
        if r == len(rounds) - 1:
            prepare_faces()
            for h in range(1, LOC_LEVELS):
                couple_level(h)
            near_steps(LEAVES_DEV // 2, LEAVES_DEV + 2)
        for copy in copies:
            copy.wait()
        nodes = [current]
        for k in range(1, 1 << bits):
            got = gathered[r, k]
            turned = pltpu.roll(got, RANK, 1)
            low = lane_high[: RHS // 2]
            nodes.append(
                jnp.concatenate(
                    [jnp.where(low, turned, got), jnp.where(low, got, turned)], axis=0
                )
            )
        for step in range(base, base + bits):
            own_half = half == ((me >> step) & 1)
            top_field.append(apply(jnp.where(own_half, nodes[1], 0.0), top_field_w[step]))
            if step + 1 < levels_top:
                is_left = half == ((me >> step) & 1)
                joined = [
                    jnp.where(is_left, nodes[2 * j], nodes[2 * j + 1])
                    for j in range(len(nodes) // 2)
                ]
                out = apply(jnp.concatenate(joined, axis=0), top_up_w[step])
                nodes = [out[RHS * j : RHS * (j + 1)] for j in range(len(joined))]
                current = nodes[0]

    spread = jnp.where(half == 0, top_field[-1], 0.0)
    for step in reversed(range(levels_top - 1)):
        out = apply(spread, top_down_w[step])
        spread = jnp.where(half == ((me >> step) & 1), out + top_field[step], 0.0)
    out = times(spread, root_twice)
    down[PAIR_AT[LOC_LEVELS - 1]] = out + field[PAIR_AT[LOC_LEVELS - 1]]

    def apart(pair):
        return jnp.concatenate(
            [jnp.where(lane_high, 0.0, pair), jnp.where(lane_high, pair, 0.0)], axis=0
        )

    for h in range(LOC_LEVELS - 1, 0, -1):

        def descend(j, _, h=h):
            weights = transfer[pl.ds(TRANSFER_AT[h] + 2 * j, 2)].reshape(2 * RANK, 2 * RANK)
            out = times(apart(down[PAIR_AT[h] + j]), weights)
            below = PAIR_AT[h - 1] + 2 * j
            down[below] = out[:RHS] + field[below]
            down[below + 1] = out[RHS:] + field[below + 1]
            return 0

        total = COUNTS[h] // 2
        lax.fori_loop(0, total, descend, 0, unroll=min(UNROLL, total))

    def expand(j, _):
        at = pl.multiple_of(j * 2 * LEAF_PTS, 2 * LEAF_PTS)
        v = basis[:, pl.ds(at, 2 * LEAF_PTS)]
        out = times(
            apart(down[j]), jnp.concatenate([v[:, :LEAF_PTS], v[:, LEAF_PTS:]], axis=0)
        )
        far[:, pl.ds(at, LEAF_PTS)] += out[:RHS]
        far[:, pl.ds(at + LEAF_PTS, LEAF_PTS)] += out[RHS:]
        return 0

    lax.fori_loop(0, LEAVES_DEV // 2, expand, 0, unroll=UNROLL)


def product_of(
    devices,
    values,
    points,
    basis,
    transfer,
    coupling,
    top_transfer,
    top_coupling,
    partners,
    columns,
    counts,
):
    leaf_points = LEAVES_DEV * LEAF_PTS
    rounds = rounds_of(devices)
    width = 1 << ROUND_BITS
    return pl.pallas_call(
        functools.partial(kernel, devices),
        out_shape=jax.ShapeDtypeStruct((RHS, leaf_points), f32),
        in_specs=[pl.BlockSpec(memory_space=pl.ANY)] * 7
        + [pl.BlockSpec(memory_space=pltpu.SMEM)] * 3,
        out_specs=pl.BlockSpec(memory_space=pltpu.VMEM),
        scratch_shapes=[
            pltpu.VMEM((2, FACE, RHS, LEAF_PTS), f32),
            pltpu.VMEM((2, 3, FACE, LEAF_PTS), f32),
            pltpu.VMEM((RHS, leaf_points), f32),
            pltpu.VMEM((3, leaf_points), f32),
            pltpu.VMEM((RANK, leaf_points), f32),
            pltpu.VMEM(transfer.shape, f32),
            pltpu.VMEM(coupling.shape, f32),
            pltpu.VMEM(top_transfer.shape, f32),
            pltpu.VMEM(top_coupling.shape, f32),
            pltpu.VMEM((2, FACE, RHS, LEAF_PTS), f32),
            pltpu.VMEM((2, 3, FACE, LEAF_PTS), f32),
            pltpu.VMEM((LEAVES_DEV - 1, RHS, 2 * RANK), f32),
            pltpu.VMEM((2, sum(RIM_PAIRS), RHS, 2 * RANK), f32),
            pltpu.VMEM((WIDE_AT[-1], RHS, 2 * RANK), f32),
            pltpu.VMEM((LEAVES_DEV - 1, RHS, 2 * RANK), f32),
            pltpu.VMEM((LEAVES_DEV - 1, RHS, 2 * RANK), f32),
            pltpu.VMEM((len(rounds), RHS // 2, 2 * RANK), f32),
            pltpu.VMEM((len(rounds), width, RHS // 2, 2 * RANK), f32),
            pltpu.VMEM((top_transfer.shape[0], 4 * RANK, 2 * RANK), bf16),
            pltpu.VMEM((top_transfer.shape[0], 4 * RANK, 2 * RANK), bf16),
            pltpu.VMEM((top_coupling.shape[0], 4 * RANK, 2 * RANK), bf16),
            pltpu.VMEM((16, SOURCES * LEAF_PTS), f32),
            pltpu.VMEM((LEAVES_DEV, TERMS, LEAF_PTS), bf16),
            pltpu.VMEM((SOURCES, LEAF_PTS, TERMS), bf16),
            pltpu.VMEM((SOURCES + 1, 2 * RHS, LEAF_PTS), bf16),
            pltpu.VMEM((2, NEAR_SLOTS // 2, 2 * LEAF_PTS, LEAF_PTS), f32),
            pltpu.VMEM((2, NEAR_SLOTS * LEAF_PTS, LEAF_PTS), bf16),
            pltpu.VMEM((2, NEAR_SLOTS * LEAF_PTS, LEAF_PTS), bf16),
            pltpu.SemaphoreType.DMA((7,)),
            pltpu.SemaphoreType.DMA((2, 2)),
            pltpu.SemaphoreType.DMA((2, 2)),
            pltpu.SemaphoreType.DMA((2, LOC_LEVELS)),
            pltpu.SemaphoreType.DMA((2, LOC_LEVELS)),
            pltpu.SemaphoreType.DMA((len(rounds), width)),
            pltpu.SemaphoreType.DMA((len(rounds), width)),
        ],
        compiler_params=pltpu.CompilerParams(
            collective_id=0, has_side_effects=True, vmem_limit_bytes=60 << 20
        ),
        name="h2_product",
    )(
        values,
        points,
        basis,
        transfer,
        coupling,
        top_transfer,
        top_coupling,
        partners,
        columns,
        counts,
    )


def local(
    values,
    points,
    basis,
    local_transfer,
    local_coupling,
    local_partners,
    top_transfer,
    top_coupling,
    near_cols,
    near_count,
):
    devices = lax.axis_size("leaf")
    return product_of(
        devices,
        values,
        points,
        basis,
        local_transfer,
        local_coupling,
        top_transfer,
        top_coupling,
        local_partners.T,
        near_cols.T,
        near_count,
    )


def solution(mesh):
    placed = (
        P(None, "leaf"),
        P(None, "leaf"),
        P(None, "leaf"),
        P("leaf", None, None),
        P("leaf", None, None),
        P("leaf", None),
        P(),
        P(),
        P("leaf", None),
        P("leaf"),
    )
    return jax.shard_map(
        local, mesh=mesh, in_specs=placed, out_specs=P(None, "leaf"), check_vma=False
    )
```

```python
import functools
import math

import jax
import jax.numpy as jnp
import numpy as np
from jax import lax
from jax.experimental import pallas as pl
from jax.experimental.pallas import tpu as pltpu
from jax.sharding import PartitionSpec as P

LEAF_PTS = 128
RANK = 64
RHS = 32
NEAR_SLOTS = 8
COUPLE = 2
WINDOW = 4
LOC_LEVELS = 6
LEAVES_DEV = 64
FACE = 16
SOURCES = LEAVES_DEV + 2 * FACE
ROUND_BITS = 4
TERMS = 32
UNROLL = 16

MESH = pl.DeviceIdType.MESH
bf16 = jnp.bfloat16
f32 = jnp.float32
LOG2E = 1.4426950408889634
SCALE = math.sqrt(3.0) / 0.5 * LOG2E
AMPLITUDE = 0.25 / LOG2E

COUNTS = [LEAVES_DEV >> h for h in range(LOC_LEVELS + 1)]
RIMS = [min(WINDOW, (LEAVES_DEV >> h) // 2) for h in range(LOC_LEVELS)]
PAIR_AT = [LEAVES_DEV - COUNTS[h] for h in range(LOC_LEVELS)]
RIM_PAIRS = [max(1, r // 2) for r in RIMS]
RIM_AT = [sum(RIM_PAIRS[:h]) for h in range(LOC_LEVELS)]
WIDE_AT = [sum(COUNTS[g] + 2 * RIMS[g] for g in range(h)) for h in range(LOC_LEVELS + 1)]
TRANSFER_AT = [LEAVES_DEV - 2 * c for c in COUNTS]
COUPLING_AT = [2 * LEAVES_DEV - 2 * c for c in COUNTS]


def rounds_of(devices):
    total = devices.bit_length() - 1
    return [(b, min(ROUND_BITS, total - b)) for b in range(0, total, ROUND_BITS)]


def halves(a):
    high = a.astype(bf16)
    return high, (a - high.astype(f32)).astype(bf16)


def doubled(left):
    high, low = halves(left)
    return jnp.concatenate(
        [
            jnp.concatenate([high, high], axis=1),
            jnp.concatenate([low, jnp.zeros_like(low)], axis=1),
        ],
        axis=0,
    )


def apply(left, stacked):
    rows = left.shape[0]
    out = jnp.dot(doubled(left), stacked, preferred_element_type=f32)
    return out[:rows] + out[rows:]


def times(left, right):
    return apply(left, jnp.concatenate(halves(right), axis=0))


def times_t(left, right):
    rows = left.shape[0]
    out = lax.dot_general(
        doubled(left),
        jnp.concatenate(halves(right), axis=1),
        (((1,), (1,)), ((), ())),
        preferred_element_type=f32,
    )
    return out[:rows] + out[rows:]


def face_leaf(side, e):
    spread = ((e & 3) << 1) | ((e >> 2) << 4)
    return spread + 9 * side


def kernel(
    devices,
    values_h,
    points_h,
    basis_h,
    transfer_h,
    coupling_h,
    top_transfer_h,
    top_coupling_h,
    partners,
    columns,
    counts,
    far,
    halo_x,
    halo_p,
    values,
    points,
    basis,
    transfer,
    coupling,
    top_transfer,
    top_coupling,
    face_x,
    face_p,
    pairs,
    rim,
    wide,
    field,
    down,
    packed,
    gathered,
    top_up_w,
    top_down_w,
    top_field_w,
    parts,
    target,
    source,
    rhs,
    squares,
    entries_high,
    entries_low,
    load_sem,
    face_send,
    face_recv,
    rim_ssem,
    rim_rsem,
    top_send,
    top_recv,
):
    me = lax.axis_index("leaf")
    right = lax.rem(me + 1, devices)
    left = lax.rem(me + devices - 1, devices)
    rounds = rounds_of(devices)
    levels_top = devices.bit_length() - 1

    barrier = pltpu.get_barrier_semaphore()
    greeted = 0
    for other in (left, right):
        pl.semaphore_signal(barrier, inc=1, device_id=(other,), device_id_type=MESH)
        greeted += 1
    for base, bits in rounds:
        for k in range(1, 1 << bits):
            pl.semaphore_signal(
                barrier, inc=1, device_id=(me ^ (k << base),), device_id_type=MESH
            )
            greeted += 1

    loads = {}
    for n, (name, src, dst) in enumerate(
        [
            ("top_transfer", top_transfer_h, top_transfer),
            ("top_coupling", top_coupling_h, top_coupling),
            ("values", values_h, values),
            ("basis", basis_h, basis),
            ("points", points_h, points),
            ("transfer", transfer_h, transfer),
            ("coupling", coupling_h, coupling),
        ]
    ):
        loads[name] = pltpu.make_async_copy(src, dst, load_sem.at[n])
        loads[name].start()

    lane_high = lax.broadcasted_iota(jnp.int32, (RHS, 2 * RANK), 1) >= RANK

    def join(out):
        return jnp.where(lane_high, out[RHS:], out[:RHS])

    def store_split(ref, at, matrix):
        high, low = halves(matrix)
        ref[at, : 2 * RANK] = high
        ref[at, 2 * RANK :] = low

    loads["top_transfer"].wait()
    loads["top_coupling"].wait()
    for step in range(levels_top):
        block = top_coupling[step]
        store_split(top_field_w, step, jnp.concatenate([block, block], axis=0).T)
        if step + 1 < levels_top:
            block = top_transfer[step]
            twice = jnp.concatenate([block, block], axis=0)
            store_split(top_up_w, step, twice.T)
            store_split(top_down_w, step, twice)

    rim_copies = [[] for _ in range(LOC_LEVELS)]

    def send_rim(h):
        count = RIM_PAIRS[h]
        at = RIM_AT[h]
        first = PAIR_AT[h]
        last = first + COUNTS[h] // 2 - count
        for side, (other, start) in enumerate(((right, last), (left, first))):
            copy = pltpu.make_async_remote_copy(
                src_ref=pairs.at[pl.ds(start, count)],
                dst_ref=rim.at[side, pl.ds(at, count)],
                send_sem=rim_ssem.at[side, h],
                recv_sem=rim_rsem.at[side, h],
                device_id=(other,),
                device_id_type=MESH,
            )
            copy.start()
            rim_copies[h].append(copy)

    def widen(h, slot, pair, which):
        turned = pltpu.roll(pair, RANK, 1)
        if which != 1:
            wide[WIDE_AT[h] + slot] = jnp.where(lane_high, turned, pair)
        if which != 0:
            wide[WIDE_AT[h] + slot + (which == 2)] = jnp.where(lane_high, pair, turned)

    loads["values"].wait()
    loads["basis"].wait()

    def leaf_pair(j, _):
        at = pl.multiple_of(j * 2 * LEAF_PTS, 2 * LEAF_PTS)
        x = values[:, pl.ds(at, 2 * LEAF_PTS)]
        v = basis[:, pl.ds(at, 2 * LEAF_PTS)]
        out = times_t(
            jnp.concatenate([x[:, :LEAF_PTS], x[:, LEAF_PTS:]], axis=0),
            jnp.concatenate([v[:, :LEAF_PTS], v[:, LEAF_PTS:]], axis=0),
        )
        pair = join(out)
        pairs[j] = pair
        widen(0, RIMS[0] + 2 * j, pair, 2)
        return 0

    lax.fori_loop(0, LEAVES_DEV // 2, leaf_pair, 0, unroll=UNROLL)
    loads["points"].wait()
    for side in range(2):
        for e in range(FACE):
            leaf = face_leaf(1 - side, e)
            at = leaf * LEAF_PTS
            face_x[side, e] = values[:, at : at + LEAF_PTS]
            for axis in range(3):
                face_p[side, axis, e : e + 1, :] = points[axis : axis + 1, at : at + LEAF_PTS]
    loads["transfer"].wait()
    for h in range(1, LOC_LEVELS):

        def node_pair(j, _, h=h):
            below = pairs[pl.ds(PAIR_AT[h - 1] + 2 * j, 2)].reshape(2 * RHS, 2 * RANK)
            weights = transfer[pl.ds(TRANSFER_AT[h] + 2 * j, 2)].reshape(2 * RANK, 2 * RANK)
            pair = join(times_t(below, weights))
            pairs[PAIR_AT[h] + j] = pair
            widen(h, RIMS[h] + 2 * j, pair, 2)
            return 0

        total = COUNTS[h] // 2
        lax.fori_loop(0, total, node_pair, 0, unroll=min(UNROLL, total))
    root = transfer[LEAVES_DEV - 2]
    root_twice = jnp.concatenate([root, root], axis=0)
    current = times_t(pairs[PAIR_AT[LOC_LEVELS - 1]], root_twice)

    def couple_level(h):
        for copy in rim_copies[h]:
            copy.wait()
        if RIMS[h] == 1:
            widen(h, 0, rim[0, RIM_AT[h]], 1)
            widen(h, 1 + COUNTS[h], rim[1, RIM_AT[h]], 0)
        else:
            for n in range(RIM_PAIRS[h]):
                widen(h, 2 * n, rim[0, RIM_AT[h] + n], 2)
                widen(h, RIMS[h] + COUNTS[h] + 2 * n, rim[1, RIM_AT[h] + n], 2)

        def couple(j, _, h=h):
            start = RIMS[h] - me * COUNTS[h]
            last = COUNTS[h] + 2 * RIMS[h] - 1
            rows = []
            for n in range(2):
                k = COUPLING_AT[h] + 2 * j + n
                first = wide[WIDE_AT[h] + jnp.clip(partners[0, k] + start, 0, last)]
                second = wide[WIDE_AT[h] + jnp.clip(partners[1, k] + start, 0, last)]
                rows.append(jnp.where(lane_high, second, first))
            weights = coupling[pl.ds(COUPLING_AT[h] + 2 * j, 2)].reshape(2 * RANK, 2 * RANK)
            field[PAIR_AT[h] + j] = join(times_t(jnp.concatenate(rows, axis=0), weights))
            return 0

        total = COUNTS[h] // 2
        lax.fori_loop(0, total, couple, 0, unroll=min(UNROLL, total))

    def three(a):
        high = a.astype(bf16).astype(f32)
        rest = a - high
        mid = rest.astype(bf16).astype(f32)
        return high, mid, rest - mid

    def lay_parts(at, width, coords):
        lanes = pl.ds(at, width)
        square = coords * coords
        norm = three(square[0:1] + square[1:2] + square[2:3])
        for n, part in enumerate(three(coords)):
            parts[3 * n : 3 * n + 3, lanes] = part
            parts[9 + n : 10 + n, lanes] = norm[n]

    def chosen(shape, row_dim, pairs_of):
        row = lax.broadcasted_iota(jnp.int32, shape, row_dim)
        term = lax.broadcasted_iota(jnp.int32, shape, 1 - row_dim)
        out = jnp.zeros(shape, f32)
        for k, (r, factor) in pairs_of.items():
            out = jnp.where((term == k) & (row == r), factor, out)
        return out.astype(bf16)

    of_target, of_source = {}, {}
    for axis in range(3):
        for n, (s, t) in enumerate(((0, 0), (0, 1), (1, 0), (0, 2), (2, 0), (1, 1))):
            of_source[3 * n + axis] = (3 * s + axis, 1.0)
            of_target[3 * n + axis] = (3 * t + axis, -2.0)
        of_source[18 + axis] = (9 + axis, 1.0)
        of_target[18 + axis] = (12, 1.0)
        of_source[21 + axis] = (12, 1.0)
        of_target[21 + axis] = (9 + axis, 1.0)

    axis_id = lax.broadcasted_iota(jnp.int32, (3, 1), 0)
    centre = jnp.where(axis_id == 0, (me * 4 + 2).astype(f32), 2.0)

    def lay_source(n):
        at = pl.multiple_of(n * LEAF_PTS, LEAF_PTS)
        turned = parts[:, pl.ds(at, LEAF_PTS)].T.astype(bf16)
        pick = chosen((16, TERMS), 0, of_source)
        source[n] = jnp.dot(turned, pick, preferred_element_type=f32).astype(bf16)

    def lay_rhs(n, x):
        high, low = halves(x)
        rhs[n, :RHS] = high
        rhs[n, RHS:] = low

    def prepare_own():
        parts[12:16, :] = jnp.where(
            lax.broadcasted_iota(jnp.int32, (4, SOURCES * LEAF_PTS), 0) == 0, 1.0, 0.0
        )
        lay_parts(0, LEAVES_DEV * LEAF_PTS, (points[...] - centre) * SCALE)
        rhs[SOURCES] = jnp.zeros((2 * RHS, LEAF_PTS), bf16)
        squares[...] = jnp.zeros_like(squares)
        entries_high[...] = jnp.zeros_like(entries_high)
        entries_low[...] = jnp.zeros_like(entries_low)

        def one(n, _):
            lanes = pl.ds(pl.multiple_of(n * LEAF_PTS, LEAF_PTS), LEAF_PTS)
            pick = chosen((TERMS, 16), 1, of_target)
            terms = jnp.dot(pick, parts[:, lanes].astype(bf16), preferred_element_type=f32)
            target[n] = terms.astype(bf16)
            lay_source(n)
            lay_rhs(n, values[:, lanes])
            return 0

        lax.fori_loop(0, LEAVES_DEV, one, 0, unroll=UNROLL)

    def prepare_faces():
        for copy in face_copies:
            copy.wait()
        for side in range(2):
            for e in range(FACE):
                at = (LEAVES_DEV + side * FACE + e) * LEAF_PTS
                coords = jnp.concatenate(
                    [halo_p[side, axis, e : e + 1, :] for axis in range(3)], axis=0
                )
                lay_parts(at, LEAF_PTS, (coords - centre) * SCALE)

        def one(e, _):
            for side in range(2):
                lay_source(LEAVES_DEV + side * FACE + e)
                lay_rhs(LEAVES_DEV + side * FACE + e, halo_x[side, e])
            return 0

        lax.fori_loop(0, FACE, one, 0, unroll=UNROLL // 2)

    def leaf_at(i):
        side = (i >> 4) & 1
        inside = jnp.where(side == 0, 1, 8)
        return face_leaf(0, i & 15) + jnp.where(i < LEAVES_DEV // 2, inside, 9 * side)

    def slot_source(leaf, slot):
        column = columns[slot, leaf] - me * LEAVES_DEV
        inner = column & (LEAVES_DEV - 1)
        face = ((inner >> 1) & 3) | (((inner >> 4) & 3) << 2)
        beyond = jnp.where(column < 0, LEAVES_DEV + face, LEAVES_DEV + FACE + face)
        return jnp.where((column >= 0) & (column < LEAVES_DEV), column, beyond)

    def near_step(i, now, later):
        done = leaf_at(jnp.maximum(i - 2, 0))
        live = counts[done]
        total = None
        for p in range(NEAR_SLOTS // 2):
            x = jnp.concatenate(
                [
                    rhs[jnp.where(slot < live, slot_source(done, slot), SOURCES)]
                    for slot in (2 * p, 2 * p + 1)
                ],
                axis=1,
            )
            rows = slice(2 * p * LEAF_PTS, 2 * (p + 1) * LEAF_PTS)
            both = jnp.dot(x, entries_high[now, rows], preferred_element_type=f32)
            rest = jnp.dot(x[:RHS], entries_low[now, rows], preferred_element_type=f32)
            out = both[:RHS] + (both[RHS:] + rest)
            total = out if total is None else total + out
        for p in range(NEAR_SLOTS // 2):
            square = jnp.maximum(squares[now, p], 1e-12)
            t = square * lax.rsqrt(square)
            high, low = halves((t + LOG2E) * jnp.exp2(-t))
            rows = slice(2 * p * LEAF_PTS, 2 * (p + 1) * LEAF_PTS)
            entries_high[later, rows] = high
            entries_low[later, rows] = low
        leaf = leaf_at(jnp.minimum(i, LEAVES_DEV - 1))
        left = jnp.concatenate(
            [source[slot_source(leaf, slot)] for slot in range(NEAR_SLOTS)], axis=0
        )
        out = jnp.dot(left, target[leaf], preferred_element_type=f32)
        for p in range(NEAR_SLOTS // 2):
            squares[later, p] = out[2 * p * LEAF_PTS : 2 * (p + 1) * LEAF_PTS]
        at = pl.multiple_of(done * LEAF_PTS, LEAF_PTS)
        far[:, pl.ds(at, LEAF_PTS)] = AMPLITUDE * total

    def near_steps(first, last):
        def two(j, _):
            near_step(2 * j, 0, 1)
            near_step(2 * j + 1, 1, 0)
            return 0

        lax.fori_loop(first // 2, last // 2, two, 0)

    half = (lax.broadcasted_iota(jnp.int32, (RHS, 2 * RANK), 1) >= RANK).astype(jnp.int32)
    top_field = []
    prepare_own()
    pl.semaphore_wait(barrier, greeted)
    face_copies = []
    for r, (base, bits) in enumerate(rounds):
        packed[r] = jnp.where(lane_high[: RHS // 2], current[RHS // 2 :], current[: RHS // 2])
        copies = []
        for k in range(1, 1 << bits):
            copy = pltpu.make_async_remote_copy(
                src_ref=packed.at[r],
                dst_ref=gathered.at[r, k],
                send_sem=top_send.at[r, k],
                recv_sem=top_recv.at[r, k],
                device_id=(me ^ (k << base),),
                device_id_type=MESH,
            )
            copy.start()
            copies.append(copy)
        if r == 0:
            for h in range(LOC_LEVELS):
                send_rim(h)
            for side, other in ((0, right), (1, left)):
                for n, (src, dst) in enumerate(((face_x, halo_x), (face_p, halo_p))):
                    copy = pltpu.make_async_remote_copy(
                        src_ref=src.at[side],
                        dst_ref=dst.at[side],
                        send_sem=face_send.at[side, n],
                        recv_sem=face_recv.at[side, n],
                        device_id=(other,),
                        device_id_type=MESH,
                    )
                    copy.start()
                    face_copies.append(copy)

            near_steps(0, LEAVES_DEV // 2)
        if r == len(rounds) - 1:
            loads["coupling"].wait()
            for h in range(LOC_LEVELS):
                couple_level(h)
            prepare_faces()
            near_steps(LEAVES_DEV // 2, LEAVES_DEV + 2)
        for copy in copies:
            copy.wait()
        nodes = [current]
        for k in range(1, 1 << bits):
            got = gathered[r, k]
            turned = pltpu.roll(got, RANK, 1)
            low = lane_high[: RHS // 2]
            nodes.append(
                jnp.concatenate(
                    [jnp.where(low, turned, got), jnp.where(low, got, turned)], axis=0
                )
            )
        for step in range(base, base + bits):
            own_half = half == ((me >> step) & 1)
            top_field.append(apply(jnp.where(own_half, nodes[1], 0.0), top_field_w[step]))
            if step + 1 < levels_top:
                is_left = half == ((me >> step) & 1)
                joined = [
                    jnp.where(is_left, nodes[2 * j], nodes[2 * j + 1])
                    for j in range(len(nodes) // 2)
                ]
                out = apply(jnp.concatenate(joined, axis=0), top_up_w[step])
                nodes = [out[RHS * j : RHS * (j + 1)] for j in range(len(joined))]
                current = nodes[0]

    spread = jnp.where(half == 0, top_field[-1], 0.0)
    for step in reversed(range(levels_top - 1)):
        out = apply(spread, top_down_w[step])
        spread = jnp.where(half == ((me >> step) & 1), out + top_field[step], 0.0)
    out = times(spread, root_twice)
    down[PAIR_AT[LOC_LEVELS - 1]] = out + field[PAIR_AT[LOC_LEVELS - 1]]

    def apart(pair):
        return jnp.concatenate(
            [jnp.where(lane_high, 0.0, pair), jnp.where(lane_high, pair, 0.0)], axis=0
        )

    for h in range(LOC_LEVELS - 1, 0, -1):

        def descend(j, _, h=h):
            weights = transfer[pl.ds(TRANSFER_AT[h] + 2 * j, 2)].reshape(2 * RANK, 2 * RANK)
            out = times(apart(down[PAIR_AT[h] + j]), weights)
            below = PAIR_AT[h - 1] + 2 * j
            down[below] = out[:RHS] + field[below]
            down[below + 1] = out[RHS:] + field[below + 1]
            return 0

        total = COUNTS[h] // 2
        lax.fori_loop(0, total, descend, 0, unroll=min(UNROLL, total))

    def expand(j, _):
        at = pl.multiple_of(j * 2 * LEAF_PTS, 2 * LEAF_PTS)
        v = basis[:, pl.ds(at, 2 * LEAF_PTS)]
        out = times(
            apart(down[j]), jnp.concatenate([v[:, :LEAF_PTS], v[:, LEAF_PTS:]], axis=0)
        )
        far[:, pl.ds(at, LEAF_PTS)] += out[:RHS]
        far[:, pl.ds(at + LEAF_PTS, LEAF_PTS)] += out[RHS:]
        return 0

    lax.fori_loop(0, LEAVES_DEV // 2, expand, 0, unroll=UNROLL)


def product_of(
    devices,
    values,
    points,
    basis,
    transfer,
    coupling,
    top_transfer,
    top_coupling,
    partners,
    columns,
    counts,
):
    leaf_points = LEAVES_DEV * LEAF_PTS
    rounds = rounds_of(devices)
    width = 1 << ROUND_BITS
    return pl.pallas_call(
        functools.partial(kernel, devices),
        out_shape=jax.ShapeDtypeStruct((RHS, leaf_points), f32),
        in_specs=[pl.BlockSpec(memory_space=pl.ANY)] * 7
        + [pl.BlockSpec(memory_space=pltpu.SMEM)] * 3,
        out_specs=pl.BlockSpec(memory_space=pltpu.VMEM),
        scratch_shapes=[
            pltpu.VMEM((2, FACE, RHS, LEAF_PTS), f32),
            pltpu.VMEM((2, 3, FACE, LEAF_PTS), f32),
            pltpu.VMEM((RHS, leaf_points), f32),
            pltpu.VMEM((3, leaf_points), f32),
            pltpu.VMEM((RANK, leaf_points), f32),
            pltpu.VMEM(transfer.shape, f32),
            pltpu.VMEM(coupling.shape, f32),
            pltpu.VMEM(top_transfer.shape, f32),
            pltpu.VMEM(top_coupling.shape, f32),
            pltpu.VMEM((2, FACE, RHS, LEAF_PTS), f32),
            pltpu.VMEM((2, 3, FACE, LEAF_PTS), f32),
            pltpu.VMEM((LEAVES_DEV - 1, RHS, 2 * RANK), f32),
            pltpu.VMEM((2, sum(RIM_PAIRS), RHS, 2 * RANK), f32),
            pltpu.VMEM((WIDE_AT[-1], RHS, 2 * RANK), f32),
            pltpu.VMEM((LEAVES_DEV - 1, RHS, 2 * RANK), f32),
            pltpu.VMEM((LEAVES_DEV - 1, RHS, 2 * RANK), f32),
            pltpu.VMEM((len(rounds), RHS // 2, 2 * RANK), f32),
            pltpu.VMEM((len(rounds), width, RHS // 2, 2 * RANK), f32),
            pltpu.VMEM((top_transfer.shape[0], 4 * RANK, 2 * RANK), bf16),
            pltpu.VMEM((top_transfer.shape[0], 4 * RANK, 2 * RANK), bf16),
            pltpu.VMEM((top_coupling.shape[0], 4 * RANK, 2 * RANK), bf16),
            pltpu.VMEM((16, SOURCES * LEAF_PTS), f32),
            pltpu.VMEM((LEAVES_DEV, TERMS, LEAF_PTS), bf16),
            pltpu.VMEM((SOURCES, LEAF_PTS, TERMS), bf16),
            pltpu.VMEM((SOURCES + 1, 2 * RHS, LEAF_PTS), bf16),
            pltpu.VMEM((2, NEAR_SLOTS // 2, 2 * LEAF_PTS, LEAF_PTS), f32),
            pltpu.VMEM((2, NEAR_SLOTS * LEAF_PTS, LEAF_PTS), bf16),
            pltpu.VMEM((2, NEAR_SLOTS * LEAF_PTS, LEAF_PTS), bf16),
            pltpu.SemaphoreType.DMA((7,)),
            pltpu.SemaphoreType.DMA((2, 2)),
            pltpu.SemaphoreType.DMA((2, 2)),
            pltpu.SemaphoreType.DMA((2, LOC_LEVELS)),
            pltpu.SemaphoreType.DMA((2, LOC_LEVELS)),
            pltpu.SemaphoreType.DMA((len(rounds), width)),
            pltpu.SemaphoreType.DMA((len(rounds), width)),
        ],
        compiler_params=pltpu.CompilerParams(
            collective_id=0, has_side_effects=True, vmem_limit_bytes=60 << 20
        ),
        name="h2_product",
    )(
        values,
        points,
        basis,
        transfer,
        coupling,
        top_transfer,
        top_coupling,
        partners,
        columns,
        counts,
    )


def local(
    values,
    points,
    basis,
    local_transfer,
    local_coupling,
    local_partners,
    top_transfer,
    top_coupling,
    near_cols,
    near_count,
):
    devices = lax.axis_size("leaf")
    return product_of(
        devices,
        values,
        points,
        basis,
        local_transfer,
        local_coupling,
        top_transfer,
        top_coupling,
        local_partners.T,
        near_cols.T,
        near_count,
    )


def solution(mesh):
    placed = (
        P(None, "leaf"),
        P(None, "leaf"),
        P(None, "leaf"),
        P("leaf", None, None),
        P("leaf", None, None),
        P("leaf", None),
        P(),
        P(),
        P("leaf", None),
        P("leaf"),
    )
    return jax.shard_map(
        local, mesh=mesh, in_specs=placed, out_specs=P(None, "leaf"), check_vma=False
    )
```

```python
import functools
import math

import jax
import jax.numpy as jnp
import numpy as np
from jax import lax
from jax.experimental import pallas as pl
from jax.experimental.pallas import tpu as pltpu
from jax.sharding import PartitionSpec as P

LEAF_PTS = 128
RANK = 64
RHS = 32
NEAR_SLOTS = 8
COUPLE = 2
WINDOW = 4
LOC_LEVELS = 6
LEAVES_DEV = 64
FACE = 16
SOURCES = LEAVES_DEV + 2 * FACE
ROUND_BITS = 4
TERMS = 32
UNROLL = 32

MESH = pl.DeviceIdType.MESH
bf16 = jnp.bfloat16
f32 = jnp.float32
LOG2E = 1.4426950408889634
SCALE = math.sqrt(3.0) / 0.5 * LOG2E
AMPLITUDE = 0.25 / LOG2E

COUNTS = [LEAVES_DEV >> h for h in range(LOC_LEVELS + 1)]
RIMS = [min(WINDOW, (LEAVES_DEV >> h) // 2) for h in range(LOC_LEVELS)]
PAIR_AT = [LEAVES_DEV - COUNTS[h] for h in range(LOC_LEVELS)]
RIM_PAIRS = [max(1, r // 2) for r in RIMS]
RIM_AT = [sum(RIM_PAIRS[:h]) for h in range(LOC_LEVELS)]
WIDE_AT = [sum(COUNTS[g] + 2 * RIMS[g] for g in range(h)) for h in range(LOC_LEVELS + 1)]
TRANSFER_AT = [LEAVES_DEV - 2 * c for c in COUNTS]
COUPLING_AT = [2 * LEAVES_DEV - 2 * c for c in COUNTS]


def rounds_of(devices):
    total = devices.bit_length() - 1
    return [(b, min(ROUND_BITS, total - b)) for b in range(0, total, ROUND_BITS)]


def halves(a):
    high = a.astype(bf16)
    return high, (a - high.astype(f32)).astype(bf16)


def doubled(left):
    high, low = halves(left)
    return jnp.concatenate(
        [
            jnp.concatenate([high, high], axis=1),
            jnp.concatenate([low, jnp.zeros_like(low)], axis=1),
        ],
        axis=0,
    )


def apply(left, stacked):
    rows = left.shape[0]
    out = jnp.dot(doubled(left), stacked, preferred_element_type=f32)
    return out[:rows] + out[rows:]


def times(left, right):
    return apply(left, jnp.concatenate(halves(right), axis=0))


def times_t(left, right):
    rows = left.shape[0]
    out = lax.dot_general(
        doubled(left),
        jnp.concatenate(halves(right), axis=1),
        (((1,), (1,)), ((), ())),
        preferred_element_type=f32,
    )
    return out[:rows] + out[rows:]


def face_leaf(side, e):
    spread = ((e & 3) << 1) | ((e >> 2) << 4)
    return spread + 9 * side


def kernel(
    devices,
    values_h,
    points_h,
    basis_h,
    transfer_h,
    coupling_h,
    top_transfer_h,
    top_coupling_h,
    partners,
    columns,
    counts,
    far,
    halo_x,
    halo_p,
    values,
    points,
    basis,
    transfer,
    coupling,
    top_transfer,
    top_coupling,
    face_x,
    face_p,
    pairs,
    rim,
    wide,
    field,
    down,
    packed,
    gathered,
    top_up_w,
    top_down_w,
    top_field_w,
    parts,
    target,
    source,
    rhs,
    squares,
    entries_high,
    entries_low,
    load_sem,
    face_send,
    face_recv,
    rim_ssem,
    rim_rsem,
    top_send,
    top_recv,
):
    me = lax.axis_index("leaf")
    right = lax.rem(me + 1, devices)
    left = lax.rem(me + devices - 1, devices)
    rounds = rounds_of(devices)
    levels_top = devices.bit_length() - 1

    barrier = pltpu.get_barrier_semaphore()
    greeted = 0
    for other in (left, right):
        pl.semaphore_signal(barrier, inc=1, device_id=(other,), device_id_type=MESH)
        greeted += 1
    for base, bits in rounds:
        for k in range(1, 1 << bits):
            pl.semaphore_signal(
                barrier, inc=1, device_id=(me ^ (k << base),), device_id_type=MESH
            )
            greeted += 1

    loads = {}
    for n, (name, src, dst) in enumerate(
        [
            ("top_transfer", top_transfer_h, top_transfer),
            ("top_coupling", top_coupling_h, top_coupling),
            ("values", values_h, values),
            ("basis", basis_h, basis),
            ("points", points_h, points),
            ("transfer", transfer_h, transfer),
            ("coupling", coupling_h, coupling),
        ]
    ):
        loads[name] = pltpu.make_async_copy(src, dst, load_sem.at[n])
        loads[name].start()

    lane_high = lax.broadcasted_iota(jnp.int32, (RHS, 2 * RANK), 1) >= RANK

    def join(out):
        return jnp.where(lane_high, out[RHS:], out[:RHS])

    def store_split(ref, at, matrix):
        high, low = halves(matrix)
        ref[at, : 2 * RANK] = high
        ref[at, 2 * RANK :] = low

    loads["top_transfer"].wait()
    loads["top_coupling"].wait()
    for step in range(levels_top):
        block = top_coupling[step]
        store_split(top_field_w, step, jnp.concatenate([block, block], axis=0).T)
        if step + 1 < levels_top:
            block = top_transfer[step]
            twice = jnp.concatenate([block, block], axis=0)
            store_split(top_up_w, step, twice.T)
            store_split(top_down_w, step, twice)

    rim_copies = [[] for _ in range(LOC_LEVELS)]

    def send_rim(h):
        count = RIM_PAIRS[h]
        at = RIM_AT[h]
        first = PAIR_AT[h]
        last = first + COUNTS[h] // 2 - count
        for side, (other, start) in enumerate(((right, last), (left, first))):
            copy = pltpu.make_async_remote_copy(
                src_ref=pairs.at[pl.ds(start, count)],
                dst_ref=rim.at[side, pl.ds(at, count)],
                send_sem=rim_ssem.at[side, h],
                recv_sem=rim_rsem.at[side, h],
                device_id=(other,),
                device_id_type=MESH,
            )
            copy.start()
            rim_copies[h].append(copy)

    def widen(h, slot, pair, which):
        turned = pltpu.roll(pair, RANK, 1)
        if which != 1:
            wide[WIDE_AT[h] + slot] = jnp.where(lane_high, turned, pair)
        if which != 0:
            wide[WIDE_AT[h] + slot + (which == 2)] = jnp.where(lane_high, pair, turned)

    loads["values"].wait()
    loads["basis"].wait()

    def leaf_pair(j, _):
        at = pl.multiple_of(j * 2 * LEAF_PTS, 2 * LEAF_PTS)
        x = values[:, pl.ds(at, 2 * LEAF_PTS)]
        v = basis[:, pl.ds(at, 2 * LEAF_PTS)]
        out = times_t(
            jnp.concatenate([x[:, :LEAF_PTS], x[:, LEAF_PTS:]], axis=0),
            jnp.concatenate([v[:, :LEAF_PTS], v[:, LEAF_PTS:]], axis=0),
        )
        pair = join(out)
        pairs[j] = pair
        widen(0, RIMS[0] + 2 * j, pair, 2)
        return 0

    lax.fori_loop(0, LEAVES_DEV // 2, leaf_pair, 0, unroll=UNROLL)
    loads["points"].wait()
    for side in range(2):
        for e in range(FACE):
            leaf = face_leaf(1 - side, e)
            at = leaf * LEAF_PTS
            face_x[side, e] = values[:, at : at + LEAF_PTS]
            for axis in range(3):
                face_p[side, axis, e : e + 1, :] = points[axis : axis + 1, at : at + LEAF_PTS]
    loads["transfer"].wait()
    for h in range(1, LOC_LEVELS):

        def node_pair(j, _, h=h):
            below = pairs[pl.ds(PAIR_AT[h - 1] + 2 * j, 2)].reshape(2 * RHS, 2 * RANK)
            weights = transfer[pl.ds(TRANSFER_AT[h] + 2 * j, 2)].reshape(2 * RANK, 2 * RANK)
            pair = join(times_t(below, weights))
            pairs[PAIR_AT[h] + j] = pair
            widen(h, RIMS[h] + 2 * j, pair, 2)
            return 0

        total = COUNTS[h] // 2
        lax.fori_loop(0, total, node_pair, 0, unroll=min(UNROLL, total))
    root = transfer[LEAVES_DEV - 2]
    root_twice = jnp.concatenate([root, root], axis=0)
    current = times_t(pairs[PAIR_AT[LOC_LEVELS - 1]], root_twice)

    def couple_level(h):
        for copy in rim_copies[h]:
            copy.wait()
        if RIMS[h] == 1:
            widen(h, 0, rim[0, RIM_AT[h]], 1)
            widen(h, 1 + COUNTS[h], rim[1, RIM_AT[h]], 0)
        else:
            for n in range(RIM_PAIRS[h]):
                widen(h, 2 * n, rim[0, RIM_AT[h] + n], 2)
                widen(h, RIMS[h] + COUNTS[h] + 2 * n, rim[1, RIM_AT[h] + n], 2)

        def couple(j, _, h=h):
            start = RIMS[h] - me * COUNTS[h]
            last = COUNTS[h] + 2 * RIMS[h] - 1
            rows = []
            for n in range(2):
                k = COUPLING_AT[h] + 2 * j + n
                first = wide[WIDE_AT[h] + jnp.clip(partners[0, k] + start, 0, last)]
                second = wide[WIDE_AT[h] + jnp.clip(partners[1, k] + start, 0, last)]
                rows.append(jnp.where(lane_high, second, first))
            weights = coupling[pl.ds(COUPLING_AT[h] + 2 * j, 2)].reshape(2 * RANK, 2 * RANK)
            field[PAIR_AT[h] + j] = join(times_t(jnp.concatenate(rows, axis=0), weights))
            return 0

        total = COUNTS[h] // 2
        lax.fori_loop(0, total, couple, 0, unroll=min(UNROLL, total))

    def three(a):
        high = a.astype(bf16).astype(f32)
        rest = a - high
        mid = rest.astype(bf16).astype(f32)
        return high, mid, rest - mid

    def lay_parts(at, width, coords):
        lanes = pl.ds(at, width)
        square = coords * coords
        norm = three(square[0:1] + square[1:2] + square[2:3])
        for n, part in enumerate(three(coords)):
            parts[3 * n : 3 * n + 3, lanes] = part
            parts[9 + n : 10 + n, lanes] = norm[n]

    def chosen(shape, row_dim, pairs_of):
        row = lax.broadcasted_iota(jnp.int32, shape, row_dim)
        term = lax.broadcasted_iota(jnp.int32, shape, 1 - row_dim)
        out = jnp.zeros(shape, f32)
        for k, (r, factor) in pairs_of.items():
            out = jnp.where((term == k) & (row == r), factor, out)
        return out.astype(bf16)

    of_target, of_source = {}, {}
    for axis in range(3):
        for n, (s, t) in enumerate(((0, 0), (0, 1), (1, 0), (0, 2), (2, 0), (1, 1))):
            of_source[3 * n + axis] = (3 * s + axis, 1.0)
            of_target[3 * n + axis] = (3 * t + axis, -2.0)
        of_source[18 + axis] = (9 + axis, 1.0)
        of_target[18 + axis] = (12, 1.0)
        of_source[21 + axis] = (12, 1.0)
        of_target[21 + axis] = (9 + axis, 1.0)

    axis_id = lax.broadcasted_iota(jnp.int32, (3, 1), 0)
    centre = jnp.where(axis_id == 0, (me * 4 + 2).astype(f32), 2.0)

    def lay_source(n):
        at = pl.multiple_of(n * LEAF_PTS, LEAF_PTS)
        turned = parts[:, pl.ds(at, LEAF_PTS)].T.astype(bf16)
        pick = chosen((16, TERMS), 0, of_source)
        source[n] = jnp.dot(turned, pick, preferred_element_type=f32).astype(bf16)

    def lay_rhs(n, x):
        high, low = halves(x)
        rhs[n, :RHS] = high
        rhs[n, RHS:] = low

    def prepare_own():
        parts[12:16, :] = jnp.where(
            lax.broadcasted_iota(jnp.int32, (4, SOURCES * LEAF_PTS), 0) == 0, 1.0, 0.0
        )
        lay_parts(0, LEAVES_DEV * LEAF_PTS, (points[...] - centre) * SCALE)
        rhs[SOURCES] = jnp.zeros((2 * RHS, LEAF_PTS), bf16)
        squares[...] = jnp.zeros_like(squares)
        entries_high[...] = jnp.zeros_like(entries_high)
        entries_low[...] = jnp.zeros_like(entries_low)

        def one(n, _):
            lanes = pl.ds(pl.multiple_of(n * LEAF_PTS, LEAF_PTS), LEAF_PTS)
            pick = chosen((TERMS, 16), 1, of_target)
            terms = jnp.dot(pick, parts[:, lanes].astype(bf16), preferred_element_type=f32)
            target[n] = terms.astype(bf16)
            lay_source(n)
            lay_rhs(n, values[:, lanes])
            return 0

        lax.fori_loop(0, LEAVES_DEV, one, 0, unroll=UNROLL)

    def prepare_faces():
        for copy in face_copies:
            copy.wait()
        for side in range(2):
            for e in range(FACE):
                at = (LEAVES_DEV + side * FACE + e) * LEAF_PTS
                coords = jnp.concatenate(
                    [halo_p[side, axis, e : e + 1, :] for axis in range(3)], axis=0
                )
                lay_parts(at, LEAF_PTS, (coords - centre) * SCALE)

        def one(e, _):
            for side in range(2):
                lay_source(LEAVES_DEV + side * FACE + e)
                lay_rhs(LEAVES_DEV + side * FACE + e, halo_x[side, e])
            return 0

        lax.fori_loop(0, FACE, one, 0, unroll=UNROLL // 2)

    def leaf_at(i):
        side = (i >> 4) & 1
        inside = jnp.where(side == 0, 1, 8)
        return face_leaf(0, i & 15) + jnp.where(i < LEAVES_DEV // 2, inside, 9 * side)

    def slot_source(leaf, slot):
        column = columns[slot, leaf] - me * LEAVES_DEV
        inner = column & (LEAVES_DEV - 1)
        face = ((inner >> 1) & 3) | (((inner >> 4) & 3) << 2)
        beyond = jnp.where(column < 0, LEAVES_DEV + face, LEAVES_DEV + FACE + face)
        return jnp.where((column >= 0) & (column < LEAVES_DEV), column, beyond)

    def near_step(i, now, later):
        done = leaf_at(jnp.maximum(i - 2, 0))
        live = counts[done]
        total = None
        for p in range(NEAR_SLOTS // 2):
            x = jnp.concatenate(
                [
                    rhs[jnp.where(slot < live, slot_source(done, slot), SOURCES)]
                    for slot in (2 * p, 2 * p + 1)
                ],
                axis=1,
            )
            rows = slice(2 * p * LEAF_PTS, 2 * (p + 1) * LEAF_PTS)
            both = jnp.dot(x, entries_high[now, rows], preferred_element_type=f32)
            rest = jnp.dot(x[:RHS], entries_low[now, rows], preferred_element_type=f32)
            out = both[:RHS] + (both[RHS:] + rest)
            total = out if total is None else total + out
        for p in range(NEAR_SLOTS // 2):
            square = jnp.maximum(squares[now, p], 1e-12)
            t = square * lax.rsqrt(square)
            high, low = halves((t + LOG2E) * jnp.exp2(-t))
            rows = slice(2 * p * LEAF_PTS, 2 * (p + 1) * LEAF_PTS)
            entries_high[later, rows] = high
            entries_low[later, rows] = low
        leaf = leaf_at(jnp.minimum(i, LEAVES_DEV - 1))
        left = jnp.concatenate(
            [source[slot_source(leaf, slot)] for slot in range(NEAR_SLOTS)], axis=0
        )
        out = jnp.dot(left, target[leaf], preferred_element_type=f32)
        for p in range(NEAR_SLOTS // 2):
            squares[later, p] = out[2 * p * LEAF_PTS : 2 * (p + 1) * LEAF_PTS]
        at = pl.multiple_of(done * LEAF_PTS, LEAF_PTS)
        far[:, pl.ds(at, LEAF_PTS)] = AMPLITUDE * total

    def near_steps(first, last):
        def two(j, _):
            near_step(2 * j, 0, 1)
            near_step(2 * j + 1, 1, 0)
            return 0

        lax.fori_loop(first // 2, last // 2, two, 0)

    half = (lax.broadcasted_iota(jnp.int32, (RHS, 2 * RANK), 1) >= RANK).astype(jnp.int32)
    top_field = []
    prepare_own()
    pl.semaphore_wait(barrier, greeted)
    face_copies = []
    for r, (base, bits) in enumerate(rounds):
        packed[r] = jnp.where(lane_high[: RHS // 2], current[RHS // 2 :], current[: RHS // 2])
        copies = []
        for k in range(1, 1 << bits):
            copy = pltpu.make_async_remote_copy(
                src_ref=packed.at[r],
                dst_ref=gathered.at[r, k],
                send_sem=top_send.at[r, k],
                recv_sem=top_recv.at[r, k],
                device_id=(me ^ (k << base),),
                device_id_type=MESH,
            )
            copy.start()
            copies.append(copy)
        if r == 0:
            for h in range(LOC_LEVELS):
                send_rim(h)
            for side, other in ((0, right), (1, left)):
                for n, (src, dst) in enumerate(((face_x, halo_x), (face_p, halo_p))):
                    copy = pltpu.make_async_remote_copy(
                        src_ref=src.at[side],
                        dst_ref=dst.at[side],
                        send_sem=face_send.at[side, n],
                        recv_sem=face_recv.at[side, n],
                        device_id=(other,),
                        device_id_type=MESH,
                    )
                    copy.start()
                    face_copies.append(copy)

            near_steps(0, LEAVES_DEV // 2)
            loads["coupling"].wait()
            couple_level(0)
        if r == len(rounds) - 1:
            for h in range(1, LOC_LEVELS):
                couple_level(h)
            prepare_faces()
            near_steps(LEAVES_DEV // 2, LEAVES_DEV + 2)
        for copy in copies:
            copy.wait()
        nodes = [current]
        for k in range(1, 1 << bits):
            got = gathered[r, k]
            turned = pltpu.roll(got, RANK, 1)
            low = lane_high[: RHS // 2]
            nodes.append(
                jnp.concatenate(
                    [jnp.where(low, turned, got), jnp.where(low, got, turned)], axis=0
                )
            )
        for step in range(base, base + bits):
            own_half = half == ((me >> step) & 1)
            top_field.append(apply(jnp.where(own_half, nodes[1], 0.0), top_field_w[step]))
            if step + 1 < levels_top:
                is_left = half == ((me >> step) & 1)
                joined = [
                    jnp.where(is_left, nodes[2 * j], nodes[2 * j + 1])
                    for j in range(len(nodes) // 2)
                ]
                out = apply(jnp.concatenate(joined, axis=0), top_up_w[step])
                nodes = [out[RHS * j : RHS * (j + 1)] for j in range(len(joined))]
                current = nodes[0]

    spread = jnp.where(half == 0, top_field[-1], 0.0)
    for step in reversed(range(levels_top - 1)):
        out = apply(spread, top_down_w[step])
        spread = jnp.where(half == ((me >> step) & 1), out + top_field[step], 0.0)
    out = times(spread, root_twice)
    down[PAIR_AT[LOC_LEVELS - 1]] = out + field[PAIR_AT[LOC_LEVELS - 1]]

    def apart(pair):
        return jnp.concatenate(
            [jnp.where(lane_high, 0.0, pair), jnp.where(lane_high, pair, 0.0)], axis=0
        )

    for h in range(LOC_LEVELS - 1, 0, -1):

        def descend(j, _, h=h):
            weights = transfer[pl.ds(TRANSFER_AT[h] + 2 * j, 2)].reshape(2 * RANK, 2 * RANK)
            out = times(apart(down[PAIR_AT[h] + j]), weights)
            below = PAIR_AT[h - 1] + 2 * j
            down[below] = out[:RHS] + field[below]
            down[below + 1] = out[RHS:] + field[below + 1]
            return 0

        total = COUNTS[h] // 2
        lax.fori_loop(0, total, descend, 0, unroll=min(UNROLL, total))

    def expand(j, _):
        at = pl.multiple_of(j * 2 * LEAF_PTS, 2 * LEAF_PTS)
        v = basis[:, pl.ds(at, 2 * LEAF_PTS)]
        out = times(
            apart(down[j]), jnp.concatenate([v[:, :LEAF_PTS], v[:, LEAF_PTS:]], axis=0)
        )
        far[:, pl.ds(at, LEAF_PTS)] += out[:RHS]
        far[:, pl.ds(at + LEAF_PTS, LEAF_PTS)] += out[RHS:]
        return 0

    lax.fori_loop(0, LEAVES_DEV // 2, expand, 0, unroll=UNROLL)


def product_of(
    devices,
    values,
    points,
    basis,
    transfer,
    coupling,
    top_transfer,
    top_coupling,
    partners,
    columns,
    counts,
):
    leaf_points = LEAVES_DEV * LEAF_PTS
    rounds = rounds_of(devices)
    width = 1 << ROUND_BITS
    return pl.pallas_call(
        functools.partial(kernel, devices),
        out_shape=jax.ShapeDtypeStruct((RHS, leaf_points), f32),
        in_specs=[pl.BlockSpec(memory_space=pl.ANY)] * 7
        + [pl.BlockSpec(memory_space=pltpu.SMEM)] * 3,
        out_specs=pl.BlockSpec(memory_space=pltpu.VMEM),
        scratch_shapes=[
            pltpu.VMEM((2, FACE, RHS, LEAF_PTS), f32),
            pltpu.VMEM((2, 3, FACE, LEAF_PTS), f32),
            pltpu.VMEM((RHS, leaf_points), f32),
            pltpu.VMEM((3, leaf_points), f32),
            pltpu.VMEM((RANK, leaf_points), f32),
            pltpu.VMEM(transfer.shape, f32),
            pltpu.VMEM(coupling.shape, f32),
            pltpu.VMEM(top_transfer.shape, f32),
            pltpu.VMEM(top_coupling.shape, f32),
            pltpu.VMEM((2, FACE, RHS, LEAF_PTS), f32),
            pltpu.VMEM((2, 3, FACE, LEAF_PTS), f32),
            pltpu.VMEM((LEAVES_DEV - 1, RHS, 2 * RANK), f32),
            pltpu.VMEM((2, sum(RIM_PAIRS), RHS, 2 * RANK), f32),
            pltpu.VMEM((WIDE_AT[-1], RHS, 2 * RANK), f32),
            pltpu.VMEM((LEAVES_DEV - 1, RHS, 2 * RANK), f32),
            pltpu.VMEM((LEAVES_DEV - 1, RHS, 2 * RANK), f32),
            pltpu.VMEM((len(rounds), RHS // 2, 2 * RANK), f32),
            pltpu.VMEM((len(rounds), width, RHS // 2, 2 * RANK), f32),
            pltpu.VMEM((top_transfer.shape[0], 4 * RANK, 2 * RANK), bf16),
            pltpu.VMEM((top_transfer.shape[0], 4 * RANK, 2 * RANK), bf16),
            pltpu.VMEM((top_coupling.shape[0], 4 * RANK, 2 * RANK), bf16),
            pltpu.VMEM((16, SOURCES * LEAF_PTS), f32),
            pltpu.VMEM((LEAVES_DEV, TERMS, LEAF_PTS), bf16),
            pltpu.VMEM((SOURCES, LEAF_PTS, TERMS), bf16),
            pltpu.VMEM((SOURCES + 1, 2 * RHS, LEAF_PTS), bf16),
            pltpu.VMEM((2, NEAR_SLOTS // 2, 2 * LEAF_PTS, LEAF_PTS), f32),
            pltpu.VMEM((2, NEAR_SLOTS * LEAF_PTS, LEAF_PTS), bf16),
            pltpu.VMEM((2, NEAR_SLOTS * LEAF_PTS, LEAF_PTS), bf16),
            pltpu.SemaphoreType.DMA((7,)),
            pltpu.SemaphoreType.DMA((2, 2)),
            pltpu.SemaphoreType.DMA((2, 2)),
            pltpu.SemaphoreType.DMA((2, LOC_LEVELS)),
            pltpu.SemaphoreType.DMA((2, LOC_LEVELS)),
            pltpu.SemaphoreType.DMA((len(rounds), width)),
            pltpu.SemaphoreType.DMA((len(rounds), width)),
        ],
        compiler_params=pltpu.CompilerParams(
            collective_id=0, has_side_effects=True, vmem_limit_bytes=60 << 20
        ),
        name="h2_product",
    )(
        values,
        points,
        basis,
        transfer,
        coupling,
        top_transfer,
        top_coupling,
        partners,
        columns,
        counts,
    )


def local(
    values,
    points,
    basis,
    local_transfer,
    local_coupling,
    local_partners,
    top_transfer,
    top_coupling,
    near_cols,
    near_count,
):
    devices = lax.axis_size("leaf")
    return product_of(
        devices,
        values,
        points,
        basis,
        local_transfer,
        local_coupling,
        top_transfer,
        top_coupling,
        local_partners.T,
        near_cols.T,
        near_count,
    )


def solution(mesh):
    placed = (
        P(None, "leaf"),
        P(None, "leaf"),
        P(None, "leaf"),
        P("leaf", None, None),
        P("leaf", None, None),
        P("leaf", None),
        P(),
        P(),
        P("leaf", None),
        P("leaf"),
    )
    return jax.shard_map(
        local, mesh=mesh, in_specs=placed, out_specs=P(None, "leaf"), check_vma=False
    )
```
